256 devices in a mesh: ctx: 16 (over z, x_lo), head: 16 (over x_hi, y, core).
Axes of the slice: x: 4 (x_hi: 2, x_lo: 2; x = x_hi * 2 + x_lo), y: 4, z: 8, core: 2. Of those that a mesh axis runs over, the one named last changes fastest.
Arguments:
- queries: bfloat16 [2048, 24576], P('ctx', 'head'), may hold values from -20 to 20
- compressed: bfloat16 [2048, 576], P('ctx'), may hold values from -60 to 60
- kv_up: bfloat16 [512, 32768], P(None, 'head'), may hold values from -0.25 to 0.25
- w_out: bfloat16 [16384, 7168], P('head', 'ctx'), may hold values from -0.046875 to 0.046875
- positions: int32 [2048], P('ctx'), may hold values from 0 to 2047, as said below
- latent_gain: float32 [512], replicated, may hold values from 0.1 to 1.9
Outputs:
- layer_out: bfloat16 [2048, 7168], P('head', 'ctx')
The draws below stay inside these ranges and needn't reach their ends.
Inputs may be any that keep to these rules, and one draw needn't show every extreme that they name: A permutation of 0 to 2047 made of runs of 64 consecutive positions, each run starting at a multiple of 64.
All inputs are finite; a program needn't handle non-finite values.
Results may differ from the reference program's by a relative error of at most 0.02.
Values may be sent and summed in bfloat16 or wider, within the bound.
A program may use at most 128 MiB of HBM per device.

```python
import math
import jax
import jax.numpy as jnp
from jax import lax

D = 7168
HEADS = 128
LAT = 512
NOPE = 128
ROPE = 64
VD = 128
TOK_DEV = 128
QK = 192
TOKENS = 2048
N_HEAD = 16


def shared_positions(key):
    half_block = TOK_DEV // 2
    block_count = TOKENS // half_block
    block_order = jax.random.permutation(jax.random.fold_in(key, 11), block_count)
    within = jnp.arange(half_block, dtype=jnp.int32)
    return (block_order.astype(jnp.int32)[:, None] * half_block + within[None, :]).reshape(-1)


def draw_positions(key, part):
    return shared_positions(key)


def draw_compressed(key, part):
    key = jax.random.fold_in(key, 3)
    first = jax.random.fold_in(key, 0)
    third = jax.random.fold_in(key, 2)
    latent = jnp.clip(jax.random.normal(first, (TOKENS, LAT), jnp.float32), -6.0, 6.0)
    rope_part = jnp.clip(jax.random.normal(third, (TOKENS, ROPE), jnp.float32), -6.0, 6.0)
    return jnp.concatenate([latent, rope_part], axis=1).astype(jnp.bfloat16)


def draw_queries(key, part):
    key = jax.random.fold_in(key, 4)
    full_draw = jnp.clip(jax.random.normal(key, (TOKENS, HEADS, QK), jnp.float32), -6.0, 6.0)
    return full_draw.reshape(TOKENS, HEADS * QK).astype(jnp.bfloat16)


def shard_levels(own_key, shape, pieces, least, top_value):
    factor_of = 1.0
    for dim, shards_of in pieces:
        draws = jax.random.uniform(jax.random.fold_in(jax.random.fold_in(own_key, 6), dim), (shards_of,), jnp.float32, least / len(pieces), top_value / len(pieces))
        factor_of = factor_of * jnp.repeat(jnp.exp(draws), shape[dim] // shards_of).reshape((-1,) + (1,) * (len(shape) - 1 - dim))
    return factor_of


def bell_draw(stream_key, extent, deviation, most, cuts=(), held_as=jnp.bfloat16):
    loudness = shard_levels(stream_key, extent, cuts, -0.22, 0.18) if cuts else 1.0
    array = jax.random.normal(stream_key, extent, jnp.float32) * deviation * loudness
    return jnp.minimum(jnp.maximum(array, -most), most).astype(held_as)


def setup_inputs(seed: int = 0) -> dict:
    streams_of = jax.random.split(jax.random.key(seed), 7)
    return {
        "queries": draw_queries(jax.random.fold_in(streams_of[6], 71), 0),
        "compressed": draw_compressed(jax.random.fold_in(streams_of[6], 71), 0),
        "kv_up": bell_draw(streams_of[2], (LAT, HEADS * (NOPE + VD)), LAT ** -0.5, 0.25, ((1, 16),)),
        "w_out": bell_draw(streams_of[3], (HEADS * VD, D), (HEADS * VD) ** -0.5, 0.046875, ((0, 16), (1, 16))),
        "positions": draw_positions(jax.random.fold_in(streams_of[6], 71), 0),
        "latent_gain": jnp.clip(1.0 + 0.18 * jax.random.normal(streams_of[5], (LAT,), jnp.float32), 0.1, 1.9),
    }


def reference(queries, compressed, kv_up, w_out, positions, latent_gain):
    latent = compressed[:, :LAT].astype(jnp.float32)
    normed = (latent * lax.rsqrt(lax.optimization_barrier(jnp.mean(latent * latent, axis=-1, keepdims=True)) + 1e-06) * latent_gain).astype(jnp.bfloat16)
    rope_wide = compressed[:, LAT:].astype(jnp.float32)
    expanded = jnp.dot(normed, kv_up, preferred_element_type=jnp.float32).astype(jnp.bfloat16)
    expanded = lax.optimization_barrier(expanded).astype(jnp.float32).reshape(TOKENS, HEADS, NOPE + VD)
    key_nope = expanded[:, :, :NOPE]
    values = expanded[:, :, NOPE:]
    query_all = queries.astype(jnp.float32).reshape(TOKENS, HEADS, QK)
    score_scale = 1.0 / math.sqrt(QK)
    block_rows = math.gcd(TOKENS, 256)

    def one_block(offset):
        query_block = lax.dynamic_slice_in_dim(query_all, offset, block_rows, 0)
        position_block = lax.dynamic_slice_in_dim(positions, offset, block_rows, 0)
        scores = jnp.einsum('qhd,khd->qhk', query_block[:, :, :NOPE], key_nope)
        scores = (scores + jnp.einsum('qhd,kd->qhk', query_block[:, :, NOPE:], rope_wide)) * score_scale
        visible = positions[None, None, :] <= position_block[:, None, None]
        scores = jnp.where(visible, scores, jnp.float32(-1e+30))
        row_max = lax.optimization_barrier(jnp.max(scores, axis=-1, keepdims=True))
        weights = jnp.exp(scores - row_max)
        totals = lax.optimization_barrier(jnp.sum(weights, axis=-1))
        rounded = lax.optimization_barrier(weights.astype(jnp.bfloat16)).astype(jnp.float32)
        mixed = jnp.einsum('qhk,khd->qhd', rounded, values) / totals[:, :, None]
        return mixed.astype(jnp.bfloat16).reshape(block_rows, HEADS * VD)
    starts = jnp.arange(0, TOKENS, block_rows, dtype=jnp.int32)
    attended = lax.map(one_block, starts).reshape(TOKENS, HEADS * VD)
    group_cols = HEADS * VD // N_HEAD

    def add_group(total, group):
        start = (group * group_cols).astype(jnp.int32)
        columns = lax.dynamic_slice_in_dim(attended, start, group_cols, 1)
        rows = lax.dynamic_slice_in_dim(w_out, start, group_cols, 0)
        partial_sum = jnp.dot(columns, rows, preferred_element_type=jnp.float32).astype(jnp.bfloat16)
        partial_sum = lax.optimization_barrier(partial_sum).astype(jnp.float32)
        return (total + partial_sum, None)
    total, unused = lax.scan(add_group, jnp.zeros((TOKENS, D), jnp.float32), jnp.arange(N_HEAD, dtype=jnp.int32))
    return total.astype(jnp.bfloat16)
```

```python
import math

import jax
import jax.numpy as jnp
from jax import lax
from jax.experimental import pallas as pl
from jax.experimental.pallas import tpu as pltpu
from jax.sharding import PartitionSpec as P

LAT = 512
NOPE = 128
ROPE = 64
VD = 128
QK = 192
WIDE = 640
ROWS = 128
HEADS_DEV = 8
CHUNKS = 4
NZ = 8
COLS = 448
MESH = pl.DeviceIdType.MESH
SCALE = 1.0 / math.sqrt(QK)
NT = (((1,), (1,)), ((), ()))


def kernel(
    q_hbm, comp_ref, kv_hbm, w_hbm, pos_ref, gain_ref, out_ref,
    packed, qcat, q_in, kv_in, kv_t, keys, vals_t, bias, att, full, w_buf, part, got1, sum1, got2, sum2, result,
    p1_send, p1_recv, p1s_send, p1s_recv, pair_send, pair_recv, w_send, w_recv, load_sem,
    ring_send, ring_recv, sib_send, sib_recv, swap_send, swap_recv,
    first_send, first_recv, second_send, second_recv, last_send, last_recv,
):
    ctx, head = lax.axis_index("ctx"), lax.axis_index("head")
    z, a = ctx // 2, ctx % 2
    xh, y, b = head // 8, (head // 2) % 4, head % 2
    x = xh * 2 + a
    diagonal = a == b
    partner = (z * 2 + b, xh * 8 + y * 2 + a)
    sibling = (ctx, xh * 8 + y * 2 + (1 - b))

    def along_z(d):
        return (((z + d + NZ) % NZ) * 2 + a, head)

    def in_plane(px, py, core):
        return (z * 2 + px % 2, (px // 2) * 8 + py * 2 + core)

    def block(dz, core):
        return ((z + dz + 2 * NZ) % NZ) * 2 + core

    def rows(blk):
        return pl.ds(pl.multiple_of(blk * ROWS, ROWS), ROWS)

    def remote(src, dst, send, recv, device):
        return pltpu.make_async_remote_copy(
            src_ref=src, dst_ref=dst, send_sem=send, recv_sem=recv, device_id=device, device_id_type=MESH
        )

    kv_load = pltpu.make_async_copy(kv_hbm, kv_in, load_sem.at[0])
    q_load = pltpu.make_async_copy(q_hbm, q_in, load_sem.at[1])
    kv_load.start()
    q_load.start()

    bar = pltpu.get_barrier_semaphore()

    def greet(k, carry):
        n = (a * 16 + head + k) % 32
        pl.semaphore_signal(bar, inc=1, device_id=(z * 2 + n // 16, n % 16), device_id_type=MESH)
        return carry

    lax.fori_loop(1, 32, greet, 0)
    for d in (1, -1):
        pl.semaphore_signal(bar, inc=1, device_id=along_z(d), device_id_type=MESH)

    latent = comp_ref[:, :LAT].astype(jnp.float32)
    normed = latent * lax.rsqrt(jnp.mean(latent * latent, axis=-1, keepdims=True) + 1e-06) * gain_ref[...]
    own = rows(ctx)
    packed[own, :LAT] = normed.astype(jnp.bfloat16)
    pos = pos_ref[...]
    high = jnp.broadcast_to((pos >> 6).astype(jnp.float32), (ROWS, ROWS)).T
    low = jnp.broadcast_to((pos & 63).astype(jnp.float32), (ROWS, ROWS)).T
    lane = lax.broadcasted_iota(jnp.int32, (ROWS, ROWS), 1)
    rope = comp_ref[:, LAT:].astype(jnp.float32)
    rope = jnp.concatenate([rope, rope], axis=1)
    tail = jnp.where(lane < 64, rope, jnp.where(lane < 96, high, low))
    packed[own, LAT:] = tail.astype(jnp.bfloat16)

    pl.semaphore_wait(bar, 33)

    pair = remote(packed.at[own], packed.at[own], pair_send, pair_recv, partner)
    w_swap = remote(w_hbm, w_buf, w_send, w_recv, partner)
    w_load = pltpu.make_async_copy(w_hbm, w_buf, load_sem.at[2])

    def p1_ring(i, s):
        d = 1 if i == 0 else -1
        part_rows = rows(block(-d * (s - 1), b))
        return remote(packed.at[part_rows], packed.at[part_rows], p1_send.at[i, s - 1], p1_recv.at[i, s - 1], along_z(d))

    def p1_half(i):
        d = 1 if i == 0 else -1
        half = pl.ds(pl.multiple_of(block(-d * 3, b) * ROWS + i * 64, 64), 64)
        return remote(packed.at[half], packed.at[half], p1_send.at[i, 3], p1_recv.at[i, 3], along_z(d))

    def p1_sib(i, s):
        d = 1 if i == 0 else -1
        part_rows = rows(block(-d * s, b))
        return remote(packed.at[part_rows], packed.at[part_rows], p1s_send.at[i, s], p1s_recv.at[i, s], sibling)

    @pl.when(jnp.logical_not(diagonal))
    def _():
        pair.start()
        w_swap.start()

    @pl.when(diagonal)
    def _():
        w_load.start()
        p1_ring(0, 1).start()
        p1_ring(1, 1).start()

    kv_load.wait()
    for h in range(HEADS_DEV):
        kv_t[h] = kv_in[:, h * 256 + NOPE : (h + 1) * 256].astype(jnp.float32).T.astype(jnp.bfloat16)
    q_load.wait()
    for j in range(HEADS_DEV // 2):
        first = q_in[:, j * 384 : j * 384 + 128]
        second = q_in[:, j * 384 + 128 : j * 384 + 256].astype(jnp.float32)
        third = q_in[:, j * 384 + 256 : j * 384 + 384].astype(jnp.float32)
        second_turned = pltpu.roll(second, 64, 1)
        third_turned = pltpu.roll(third, 64, 1)
        qcat[2 * j, :, :NOPE] = first
        qcat[2 * j, :, NOPE:] = jnp.where(lane < 64, second, 0.0).astype(jnp.bfloat16)
        qcat[2 * j + 1, :, :NOPE] = jnp.where(lane < 64, second_turned, third_turned).astype(jnp.bfloat16)
        qcat[2 * j + 1, :, NOPE:] = jnp.where(lane < 64, third_turned, 0.0).astype(jnp.bfloat16)

    def expand(blk0, blk1):
        both = jnp.concatenate([packed[rows(blk0), :LAT], packed[rows(blk1), :LAT]], axis=0)

        def heads(hp, carry):
            k_cols = jnp.concatenate(
                [kv_in[:, pl.ds(pl.multiple_of(hp * 512 + i * 256, 256), NOPE)] for i in (0, 1)], axis=1
            )
            k = jnp.dot(both, k_cols, preferred_element_type=jnp.float32).astype(jnp.bfloat16)
            v_rows = jnp.concatenate([kv_t[hp * 2], kv_t[hp * 2 + 1]], axis=0)
            v = lax.dot_general(v_rows, both, NT, preferred_element_type=jnp.float32).astype(jnp.bfloat16)
            for i in (0, 1):
                for j, blk in ((0, blk0), (1, blk1)):
                    keys[hp * 2 + i, rows(blk), :] = k[j * 128 : j * 128 + 128, i * 128 : i * 128 + 128]
                    vals_t[hp * 2 + i, :, rows(blk)] = v[i * 128 : i * 128 + 128, j * 128 : j * 128 + 128]
            return carry

        lax.fori_loop(0, HEADS_DEV // 2, heads, 0)
        for blk in (blk0, blk1):
            extra = packed[rows(blk), LAT:].astype(jnp.float32)
            key_pos = extra[:, 64:65] * 64.0 + extra[:, 96:97]
            visible = key_pos <= pos.astype(jnp.float32)
            bias[rows(blk), :] = jnp.where(visible, 0.0, -1e30)

    @pl.when(jnp.logical_not(diagonal))
    def _():
        pair.wait_recv()
        p1_ring(0, 1).start()
        p1_ring(1, 1).start()
        p1_sib(0, 0).start()

    @pl.when(diagonal)
    def _():
        p1_sib(0, 0).wait_recv()

    expand(block(0, 0), block(0, 1))

    def p1_step(s, carry):
        for i in (0, 1):
            p1_ring(i, s).wait_recv()
            p1_sib(i, s).start()

            @pl.when(s < 3)
            def _():
                p1_ring(i, s + 1).start()

            @pl.when(s == 3)
            def _():
                p1_half(i).start()

        expand(block(-s, b), block(s, b))

        @pl.when(s > 1)
        def _():
            for i in (0, 1):
                p1_sib(i, s - 1).wait_recv()
            expand(block(1 - s, 1 - b), block(s - 1, 1 - b))

        return carry

    lax.fori_loop(1, 4, p1_step, 0)
    for i in (0, 1):
        p1_half(i).wait_recv()
    p1_sib(0, 4).start()
    for i in (0, 1):
        p1_sib(i, 3).wait_recv()
    expand(block(-3, 1 - b), block(3, 1 - b))
    p1_sib(0, 4).wait_recv()
    expand(block(4, 0), block(4, 1))

    def attend(h):
        k = jnp.concatenate([keys[h], packed[:, LAT:]], axis=1)
        s = lax.dot_general(k, qcat[h], NT, preferred_element_type=jnp.float32)
        s = s * SCALE + bias[...]
        e = jnp.exp(s - jnp.max(s, axis=0, keepdims=True))
        total = jnp.sum(e, axis=0, keepdims=True)
        o = jnp.dot(vals_t[h], e.astype(jnp.bfloat16), preferred_element_type=jnp.float32)
        return (o / total).T.astype(jnp.bfloat16)

    def ring(i, p, s):
        d = 1 if i == 0 else -1
        r = rows(block(-d * (s - 1), b))
        return remote(full.at[p, r], full.at[p, r], ring_send.at[i, p, s - 1], ring_recv.at[i, p, s - 1], along_z(d))

    def sib(p, n, dz):
        r = rows(block(dz, b))
        return remote(full.at[p, r], full.at[p, r], sib_send.at[p, n], sib_recv.at[p, n], sibling)

    def swap(p):
        return remote(att.at[p], full.at[p, own], swap_send.at[p], swap_recv.at[p], partner)

    def sib_of(p, i, s):
        d = 1 if i == 0 else -1
        return sib(p, i * 3 + s, -d * s)

    def pass_on(p, s):
        @pl.when(s < 4)
        def _():
            for i in (0, 1):
                ring(i, p, s).wait_recv()
                sib_of(p, i, s).start()

                @pl.when((s < 3) | ((p < 2) if i == 0 else (p >= 2)))
                def _():
                    ring(i, p, s + 1).start()

        @pl.when(s == 4)
        def _():
            for i in (0, 1):
                @pl.when((p < 2) if i == 0 else (p >= 2))
                def _():
                    ring(i, p, 4).wait_recv()
            sib(p, 7, 4).start()

    def early(t, carry):
        for i in (0, 1):
            att[t, :, i * VD : (i + 1) * VD] = attend(2 * t + i)

        @pl.when(diagonal)
        def _():
            full[t, own, :] = att[t]

        @pl.when(jnp.logical_not(diagonal))
        def _():
            swap(t).start()
            swap(t).wait_recv()

        ring(0, t, 1).start()
        ring(1, t, 1).start()
        sib(t, 0, 0).start()

        def older(p, c):
            pass_on(p, t - p)
            return c

        lax.fori_loop(0, t, older, 0)
        return carry

    lax.fori_loop(0, CHUNKS, early, 0)

    u = jnp.where(b == 0, y, x)
    v = jnp.where(b == 0, x, y)

    def first_copy(n, j):
        t = (u + j) % 4
        device = in_plane(jnp.where(b == 0, x, t), jnp.where(b == 0, t, y), b)
        src = part.at[n, pl.ds(pl.multiple_of(t * 64, 64), 64)]
        return remote(src, got1.at[n, j - 1], first_send.at[n, j - 1], first_recv.at[n, j - 1], device)

    def second_copy(n, j):
        t = (v + j) % 4
        device = in_plane(jnp.where(b == 0, t, x), jnp.where(b == 0, y, t), b)
        src = sum1.at[n, pl.ds(pl.multiple_of(t * 16, 16), 16)]
        return remote(src, got2.at[n, j - 1], second_send.at[n, j - 1], second_recv.at[n, j - 1], device)

    def far(n):
        return (z + jnp.where(n % 2 == 1, -((n + 1) // 2), n // 2) + NZ) % NZ

    def project(n, carry):
        zp = far(n)
        for i in (0, 1):
            r = rows(zp * 2 + i)
            lhs = jnp.concatenate([full[p, r, :] for p in range(CHUNKS)], axis=1)
            part[n, i * ROWS : (i + 1) * ROWS, :] = jnp.dot(
                lhs, w_buf[...], preferred_element_type=jnp.float32
            ).astype(jnp.bfloat16)
        for j in (1, 2, 3):
            first_copy(n, j).start()
        return carry

    def sum_first(n, carry):
        total = part[n, pl.ds(pl.multiple_of(u * 64, 64), 64), :].astype(jnp.float32)
        for j in (1, 2, 3):
            first_copy(n, j).wait_recv()
        for j in (1, 2, 3):
            total = total + got1[n, j - 1].astype(jnp.float32)
        sum1[n] = total.astype(jnp.bfloat16)
        for j in (1, 2, 3):
            second_copy(n, j).start()
        return carry

    slot = (u % 2) * 4 + v

    def last_copy(n):
        zp = far(n)
        device = in_plane((zp // 4) * 2 + b, zp % 4, u // 2)
        return remote(
            sum2.at[n], result.at[pl.ds(pl.multiple_of(slot * 16, 16), 16)], last_send.at[n], last_recv.at[slot], device
        )

    def stays(n):
        zp = far(n)
        return diagonal & (u // 2 == b) & (zp == xh * 4 + y)

    def sum_second(n, carry):
        total = sum1[n, pl.ds(pl.multiple_of(v * 16, 16), 16), :].astype(jnp.float32)
        for j in (1, 2, 3):
            second_copy(n, j).wait_recv()
        for j in (1, 2, 3):
            total = total + got2[n, j - 1].astype(jnp.float32)
        sum2[n] = total.astype(jnp.bfloat16)

        @pl.when(stays(n))
        def _():
            result[pl.ds(pl.multiple_of(slot * 16, 16), 16), :] = sum2[n]

        @pl.when(jnp.logical_not(stays(n)))
        def _():
            last_copy(n).start()

        return carry

    def sib_wait(i, s):
        for p in range(CHUNKS):
            sib_of(p, i, s).wait_recv()

    @pl.when(diagonal)
    def _():
        w_load.wait()

    @pl.when(jnp.logical_not(diagonal))
    def _():
        w_swap.wait_recv()

    def pass_all(t):
        def older(p, c):
            pass_on(p, t - p)
            return c

        lax.fori_loop(max(0, t - 4), CHUNKS, older, 0)

    pass_all(4)
    for p in range(CHUNKS):
        sib(p, 0, 0).wait_recv()
    project(0, 0)
    for i in (0, 1):
        sib_wait(i, 1)
    lax.fori_loop(1, 3, project, 0)
    pass_all(5)
    for i in (0, 1):
        sib_wait(i, 2)
    lax.fori_loop(3, 5, project, 0)
    lax.fori_loop(0, 3, sum_first, 0)
    pass_all(6)
    for i in (0, 1):
        sib_wait(i, 3)
    lax.fori_loop(5, 7, project, 0)
    lax.fori_loop(3, 5, sum_first, 0)
    lax.fori_loop(0, 3, sum_second, 0)
    pass_all(7)
    for p in range(CHUNKS):
        sib(p, 7, 4).wait_recv()
    project(7, 0)
    lax.fori_loop(5, 7, sum_first, 0)
    lax.fori_loop(3, 5, sum_second, 0)
    sum_first(7, 0)
    lax.fori_loop(5, 8, sum_second, 0)

    for n in range(8):
        un = b * 2 + n // 4
        mine = diagonal & (un == u) & (n % 4 == v)

        @pl.when(jnp.logical_not(mine))
        def _():
            remote(sum2.at[0], result.at[pl.ds(n * 16, 16)], last_send.at[0], last_recv.at[n], sibling).wait_recv()

    out_ref[...] = result[...]

    @pl.when(jnp.logical_not(diagonal))
    def _():
        pair.wait_send()
        w_swap.wait_send()
        p1_sib(0, 0).wait_send()
        for p in range(CHUNKS):
            swap(p).wait_send()

    for i in (0, 1):
        for s in (1, 2, 3):
            p1_ring(i, s).wait_send()
            p1_sib(i, s).wait_send()
        p1_half(i).wait_send()
    p1_sib(0, 4).wait_send()

    def drain(p, carry):
        sib(p, 0, 0).wait_send()
        sib(p, 7, 4).wait_send()
        for i in (0, 1):
            for s in (1, 2, 3):
                ring(i, p, s).wait_send()
                sib_of(p, i, s).wait_send()

            @pl.when((p < 2) if i == 0 else (p >= 2))
            def _():
                ring(i, p, 4).wait_send()

        return carry

    lax.fori_loop(0, CHUNKS, drain, 0)

    def drain_sums(n, carry):
        for j in (1, 2, 3):
            first_copy(n, j).wait_send()
            second_copy(n, j).wait_send()

        @pl.when(jnp.logical_not(stays(n)))
        def _():
            last_copy(n).wait_send()

        return carry

    lax.fori_loop(0, NZ, drain_sums, 0)


def per_device(queries, compressed, kv_up, w_out, positions, latent_gain):
    bf16, f32 = jnp.bfloat16, jnp.float32
    dma = pltpu.SemaphoreType.DMA
    any_space = pl.BlockSpec(memory_space=pl.ANY)
    vmem = pl.BlockSpec(memory_space=pltpu.VMEM)
    return pl.pallas_call(
        kernel,
        out_shape=jax.ShapeDtypeStruct((ROWS, COLS), bf16),
        in_specs=[any_space, vmem, any_space, any_space, vmem, vmem],
        out_specs=vmem,
        scratch_shapes=[
            pltpu.VMEM((NZ * 2 * ROWS, WIDE), bf16),
            pltpu.VMEM((HEADS_DEV, ROWS, 256), bf16),
            pltpu.VMEM((ROWS, HEADS_DEV * QK), bf16),
            pltpu.VMEM((LAT, HEADS_DEV * 256), bf16),
            pltpu.VMEM((HEADS_DEV, VD, LAT), bf16),
            pltpu.VMEM((HEADS_DEV, NZ * 2 * ROWS, NOPE), bf16),
            pltpu.VMEM((HEADS_DEV, VD, NZ * 2 * ROWS), bf16),
            pltpu.VMEM((NZ * 2 * ROWS, ROWS), f32),
            pltpu.VMEM((CHUNKS, ROWS, 256), bf16),
            pltpu.VMEM((CHUNKS, NZ * 2 * ROWS, 256), bf16),
            pltpu.VMEM((HEADS_DEV * VD, COLS), bf16),
            pltpu.VMEM((NZ, 2 * ROWS, COLS), bf16),
            pltpu.VMEM((NZ, 3, 64, COLS), bf16),
            pltpu.VMEM((NZ, 64, COLS), bf16),
            pltpu.VMEM((NZ, 3, 16, COLS), bf16),
            pltpu.VMEM((NZ, 16, COLS), bf16),
            pltpu.VMEM((ROWS, COLS), bf16),
            dma((2, 4)), dma((2, 4)),
            dma((2, 5)), dma((2, 5)),
            dma, dma,
            dma, dma,
            dma((3,)),
            dma((2, CHUNKS, 4)), dma((2, CHUNKS, 4)),
            dma((CHUNKS, 8)), dma((CHUNKS, 8)),
            dma((CHUNKS,)), dma((CHUNKS,)),
            dma((NZ, 3)), dma((NZ, 3)),
            dma((NZ, 3)), dma((NZ, 3)),
            dma((NZ,)), dma((NZ,)),
        ],
        compiler_params=pltpu.CompilerParams(
            collective_id=0, has_side_effects=True, vmem_limit_bytes=56 * 1024 * 1024
        ),
        name="prefill",
    )(queries, compressed, kv_up, w_out, positions.reshape(1, ROWS), latent_gain.reshape(1, LAT))


def solution(mesh):
    in_specs = (P("ctx", "head"), P("ctx", None), P(None, "head"), P("head", "ctx"), P("ctx"), P())
    return jax.shard_map(
        per_device, mesh=mesh, in_specs=in_specs, out_specs=P("head", "ctx"), check_vma=False
    )
```

```python
import math

import jax
import jax.numpy as jnp
from jax import lax
from jax.experimental import pallas as pl
from jax.experimental.pallas import tpu as pltpu
from jax.sharding import PartitionSpec as P

LAT = 512
NOPE = 128
ROPE = 64
VD = 128
QK = 192
WIDE = 640
ROWS = 128
HEADS_DEV = 8
CHUNKS = 4
NZ = 8
COLS = 448
MESH = pl.DeviceIdType.MESH
SCALE = math.log2(math.e) / math.sqrt(QK)
NT = (((1,), (1,)), ((), ()))


def kernel(
    q_hbm, comp_ref, kv_hbm, w_hbm, pos_ref, gain_ref, out_ref,
    packed, qcat, q_in, kv_in, kv_t, stats, acc, att, full, w_buf, part, got1, sum1, got2, sum2, result,
    far_send, far_recv, near_send, near_recv, half_send, half_recv,
    w_send, w_recv, load_sem,
    ring_send, ring_recv, sib_send, sib_recv, swap_send, swap_recv,
    first_send, first_recv, second_send, second_recv, last_send, last_recv,
):
    ctx, head = lax.axis_index("ctx"), lax.axis_index("head")
    z, a = ctx // 2, ctx % 2
    xh, y, b = head // 8, (head // 2) % 4, head % 2
    x = xh * 2 + a
    diagonal = a == b
    partner = (z * 2 + b, xh * 8 + y * 2 + a)
    sibling = (ctx, xh * 8 + y * 2 + (1 - b))

    def along_z(d):
        return (((z + d + NZ) % NZ) * 2 + a, head)

    def partner_z(d):
        return (((z + d + NZ) % NZ) * 2 + b, xh * 8 + y * 2 + a)

    def in_plane(px, py, core):
        return (z * 2 + px % 2, (px // 2) * 8 + py * 2 + core)

    def block(dz, core):
        return ((z + dz + 2 * NZ) % NZ) * 2 + core

    def rows(blk):
        return pl.ds(pl.multiple_of(blk * ROWS, ROWS), ROWS)

    def remote(src, dst, send, recv, device):
        return pltpu.make_async_remote_copy(
            src_ref=src, dst_ref=dst, send_sem=send, recv_sem=recv, device_id=device, device_id_type=MESH
        )

    kv_load = pltpu.make_async_copy(kv_hbm, kv_in, load_sem.at[0])
    q_load = pltpu.make_async_copy(q_hbm, q_in, load_sem.at[1])
    kv_load.start()
    q_load.start()

    bar = pltpu.get_barrier_semaphore()

    def greet(k, carry):
        n = (a * 16 + head + k) % 32
        pl.semaphore_signal(bar, inc=1, device_id=(z * 2 + n // 16, n % 16), device_id_type=MESH)
        return carry

    lax.fori_loop(1, 32, greet, 0)
    for d in range(1, NZ):
        pl.semaphore_signal(bar, inc=1, device_id=along_z(d), device_id_type=MESH)
    for d in (1, -1):

        @pl.when(jnp.logical_not(diagonal))
        def _():
            pl.semaphore_signal(bar, inc=1, device_id=partner_z(d), device_id_type=MESH)

    latent = comp_ref[:LAT, :].astype(jnp.float32).T
    normed = latent * lax.rsqrt(jnp.mean(latent * latent, axis=-1, keepdims=True) + 1e-06) * gain_ref[...]
    own = rows(ctx)
    packed[own, :LAT] = normed.astype(jnp.bfloat16)
    pos = pos_ref[...]
    high = jnp.broadcast_to((pos >> 6).astype(jnp.float32), (ROWS, ROWS)).T
    low = jnp.broadcast_to((pos & 63).astype(jnp.float32), (ROWS, ROWS)).T
    lane = lax.broadcasted_iota(jnp.int32, (ROWS, ROWS), 1)
    rope = comp_ref[LAT:, :].astype(jnp.float32)
    rope = jnp.concatenate([rope, rope], axis=0).T
    tail = jnp.where(lane < 64, rope, jnp.where(lane < 96, high, low))
    packed[own, LAT:] = tail.astype(jnp.bfloat16)

    pl.semaphore_wait(bar, jnp.where(diagonal, 38, 40))

    def far(n):
        return (z + jnp.where(n % 2 == 1, -((n + 1) // 2), n // 2) + NZ) % NZ

    w_swap = remote(w_hbm, w_buf, w_send, w_recv, partner)
    w_load = pltpu.make_async_copy(w_hbm, w_buf, load_sem.at[2])

    def piece(n, col, first, count):
        start = (far(n) * 2 + col) * ROWS + b * 64 + first
        return packed.at[pl.ds(pl.multiple_of(start, 32), count)]

    def from_far(n):
        d = (n + 1) // 2 if n % 2 == 1 else -(n // 2)
        ref = piece(0, a, (y % 2) * 32, 32)
        return remote(ref, ref, far_send.at[n], far_recv.at[n], along_z(d))

    def from_near(k, n):
        ref = piece(n, a, (y % 2) * 32, 32)
        turn = 1 - 2 * b
        device = in_plane((x + 4 + turn * (k > 0)) % 4, (y + 4 + turn * (k != 1)) % 4, b)
        return remote(ref, ref, near_send.at[k, n], near_recv.at[k, n], device)

    def half(k, n):
        ref = piece(n, 1 - a if k else a, 0, 64)
        return remote(ref, ref, half_send.at[k, n], half_recv.at[k, n], sibling)

    def go(copies):
        for copy in copies:
            copy.start()

    def arrive(copies):
        for copy in copies:
            copy.wait_recv()

    go([from_far(n) for n in range(1, NZ)])
    go([from_near(1, 0), from_near(2, 0)])

    @pl.when(jnp.logical_not(diagonal))
    def _():
        w_swap.start()

    @pl.when(diagonal)
    def _():
        w_load.start()

    kv_load.wait()
    for h in range(HEADS_DEV):
        kv_t[h] = kv_in[:, h * 256 + NOPE : (h + 1) * 256].astype(jnp.float32).T.astype(jnp.bfloat16)
    q_load.wait()
    for j in range(HEADS_DEV // 2):
        first = q_in[:, j * 384 : j * 384 + 128]
        second = q_in[:, j * 384 + 128 : j * 384 + 256].astype(jnp.float32)
        third = q_in[:, j * 384 + 256 : j * 384 + 384].astype(jnp.float32)
        second_turned = pltpu.roll(second, 64, 1)
        third_turned = pltpu.roll(third, 64, 1)
        qcat[2 * j, :, :NOPE] = first
        qcat[2 * j, :, NOPE:] = jnp.where(lane < 64, second, 0.0).astype(jnp.bfloat16)
        qcat[2 * j + 1, :, :NOPE] = jnp.where(lane < 64, second_turned, third_turned).astype(jnp.bfloat16)
        qcat[2 * j + 1, :, NOPE:] = jnp.where(lane < 64, third_turned, 0.0).astype(jnp.bfloat16)

    for h in range(HEADS_DEV):
        stats[h, 0:1, :] = jnp.full((1, ROWS), -1e30, jnp.float32)
        stats[h, 1:2, :] = jnp.zeros((1, ROWS), jnp.float32)
        acc[h] = jnp.zeros((VD, ROWS), jnp.float32)

    def attend(blk0, blk1):
        both = jnp.concatenate([packed[rows(blk0), :LAT], packed[rows(blk1), :LAT]], axis=0)
        extra = jnp.concatenate([packed[rows(blk0), LAT:], packed[rows(blk1), LAT:]], axis=0)
        wide = extra.astype(jnp.float32)
        key_pos = wide[:, 64:65] * 64.0 + wide[:, 96:97]
        bias = jnp.where(key_pos <= pos.astype(jnp.float32), 0.0, -1e30)
        heads = range(HEADS_DEV)
        ks, vs = [], []
        for hp in range(HEADS_DEV // 2):
            k_cols = jnp.concatenate([kv_in[:, hp * 512 + i * 256 : hp * 512 + i * 256 + NOPE] for i in (0, 1)], axis=1)
            ks.append(jnp.dot(both, k_cols, preferred_element_type=jnp.float32).astype(jnp.bfloat16))
            v_rows = jnp.concatenate([kv_t[hp * 2], kv_t[hp * 2 + 1]], axis=0)
            vs.append(lax.dot_general(v_rows, both, NT, preferred_element_type=jnp.float32).astype(jnp.bfloat16))
        scores = []
        for h in heads:
            k_all = jnp.concatenate([ks[h // 2][:, h % 2 * 128 : h % 2 * 128 + 128], extra], axis=1)
            scores.append(lax.dot_general(k_all, qcat[h], NT, preferred_element_type=jnp.float32) * SCALE + bias)
        exps, fades = [], []
        for h in heads:
            before = stats[h, 0:1, :]
            top = jnp.maximum(before, jnp.max(scores[h], axis=0, keepdims=True))
            fade = jnp.exp2(before - top)
            e = jnp.exp2(scores[h] - top)
            stats[h, 0:1, :] = top
            stats[h, 1:2, :] = stats[h, 1:2, :] * fade + jnp.sum(e, axis=0, keepdims=True)
            exps.append(e.astype(jnp.bfloat16))
            fades.append(fade)
        for h in heads:
            v = vs[h // 2][h % 2 * 128 : h % 2 * 128 + 128, :]
            acc[h] = acc[h] * fades[h] + jnp.dot(v, exps[h], preferred_element_type=jnp.float32)

    def from_z(*ns):
        for n in ns:
            from_far(n).wait_recv()
            go([from_near(k, n) for k in range(3)])

    def from_plane(*ns):
        for n in ns:
            arrive([from_near(k, n) for k in range(3)])
            go([half(k, n) for k in (0, 1)])

    def before_stage(g):
        if g == 0:
            arrive([from_near(1, 0), from_near(2, 0)])
            half(1, 0).start()
            from_z(1, 2)
            half(1, 0).wait_recv()
        if g == 1:
            from_z(3, 4)
            from_plane(1, 2)
        if g == 2:
            from_z(5, 6)
        if g == 3:
            from_z(7)
            from_plane(3, 4)
        if g == 4:
            from_plane(5)
        if g == 5:
            from_plane(6, 7)
        if g > 0:
            arrive([half(k, g) for k in (0, 1)])

    def stage(g, carry):
        for k in range(NZ):
            @pl.when(g == k)
            def _():
                before_stage(k)

        attend(far(g) * 2, far(g) * 2 + 1)
        return carry

    lax.fori_loop(0, NZ, stage, 0)

    def ring(i, p, s):
        d = 1 if i == 0 else -1
        r = rows(block(-d * (s - 1), b))
        return remote(full.at[p, r], full.at[p, r], ring_send.at[i, p, s - 1], ring_recv.at[i, p, s - 1], along_z(d))

    def sib(p, n, dz):
        r = rows(block(dz, b))
        return remote(full.at[p, r], full.at[p, r], sib_send.at[p, n], sib_recv.at[p, n], sibling)

    def swap(p):
        return remote(att.at[p], full.at[p, own], swap_send.at[p], swap_recv.at[p], partner)

    def sib_of(p, i, s):
        d = 1 if i == 0 else -1
        return sib(p, i * 3 + s, -d * s)

    def ring_first(i, p):
        return remote(
            att.at[p], full.at[p, own], ring_send.at[i, p, 0], ring_recv.at[i, p, 0], partner_z(1 if i == 0 else -1)
        )

    def pass_on(p, s):
        if s < 4:
            for i in (0, 1):
                ring(i, p, s).wait_recv()
                if s < 3 or i == p // 2:
                    ring(i, p, s + 1).start()
                sib_of(p, i, s).start()
        else:
            ring(p // 2, p, 4).wait_recv()
            sib(p, 7, 4).start()

    for p in range(CHUNKS):
        for i in (0, 1):
            o = acc[2 * p + i] / stats[2 * p + i, 1:2, :]
            att[p, :, i * VD : (i + 1) * VD] = o.T.astype(jnp.bfloat16)
        ring_first(0, p).start()
        ring_first(1, p).start()

        @pl.when(diagonal)
        def _():
            full[p, own, :] = att[p]
            sib(p, 0, 0).start()

        @pl.when(jnp.logical_not(diagonal))
        def _():
            swap(p).start()

    def home(chunks):
        @pl.when(jnp.logical_not(diagonal))
        def _():
            for p in chunks:
                swap(p).wait_recv()
                sib(p, 0, 0).start()

    pass_on(0, 1)
    pass_on(1, 1)
    home((0, 1, 2, 3))

    u = jnp.where(b == 0, y, x)
    v = jnp.where(b == 0, x, y)

    def first_copy(n, j):
        t = (u + j) % 4
        device = in_plane(jnp.where(b == 0, x, t), jnp.where(b == 0, t, y), b)
        src = part.at[n, pl.ds(pl.multiple_of(t * 64, 64), 64)]
        return remote(src, got1.at[n, j - 1], first_send.at[n, j - 1], first_recv.at[n, j - 1], device)

    def second_copy(n, j):
        t = (v + j) % 4
        device = in_plane(jnp.where(b == 0, t, x), jnp.where(b == 0, y, t), b)
        src = sum1.at[n, pl.ds(pl.multiple_of(t * 16, 16), 16)]
        return remote(src, got2.at[n, j - 1], second_send.at[n, j - 1], second_recv.at[n, j - 1], device)

    def project(n, carry):
        zp = far(n)
        for i in (0, 1):
            r = rows(zp * 2 + i)
            lhs = jnp.concatenate([full[p, r, :] for p in range(CHUNKS)], axis=1)
            part[n, i * ROWS : (i + 1) * ROWS, :] = lax.dot_general(
                lhs, w_buf[...], NT, preferred_element_type=jnp.float32
            ).astype(jnp.bfloat16)
        for j in (1, 2, 3):
            first_copy(n, j).start()
        return carry

    def sum_first(n, carry):
        total = part[n, pl.ds(pl.multiple_of(u * 64, 64), 64), :].astype(jnp.float32)
        for j in (1, 2, 3):
            first_copy(n, j).wait_recv()
        for j in (1, 2, 3):
            total = total + got1[n, j - 1].astype(jnp.float32)
        sum1[n] = total.astype(jnp.bfloat16)
        for j in (1, 2, 3):
            second_copy(n, j).start()
        return carry

    slot = (u % 2) * 4 + v

    def last_copy(n):
        zp = far(n)
        device = in_plane((zp // 4) * 2 + b, zp % 4, u // 2)
        return remote(
            sum2.at[n], result.at[pl.ds(pl.multiple_of(slot * 16, 16), 16)], last_send.at[n], last_recv.at[slot], device
        )

    def stays(n):
        zp = far(n)
        return diagonal & (u // 2 == b) & (zp == xh * 4 + y)

    def sum_second(n, carry):
        total = sum1[n, pl.ds(pl.multiple_of(v * 16, 16), 16), :].astype(jnp.float32)
        for j in (1, 2, 3):
            second_copy(n, j).wait_recv()
        for j in (1, 2, 3):
            total = total + got2[n, j - 1].astype(jnp.float32)
        sum2[n] = total.astype(jnp.bfloat16)

        @pl.when(stays(n))
        def _():
            result[pl.ds(pl.multiple_of(slot * 16, 16), 16), :] = sum2[n]

        @pl.when(jnp.logical_not(stays(n)))
        def _():
            last_copy(n).start()

        return carry

    def sib_wait(i, s):
        for p in range(CHUNKS):
            sib_of(p, i, s).wait_recv()

    @pl.when(diagonal)
    def _():
        w_load.wait()

    @pl.when(jnp.logical_not(diagonal))
    def _():
        w_swap.wait_recv()

    def project_round(s):
        for i in (0, 1):
            sib_wait(i, s)
        lax.fori_loop(2 * s - 1, 2 * s + 1, project, 0)

    for p in (2, 3):
        pass_on(p, 1)
    for p in range(CHUNKS):
        sib(p, 0, 0).wait_recv()
    project(0, 0)
    pass_on(0, 2)
    pass_on(1, 2)
    project_round(1)
    pass_on(2, 2)
    pass_on(3, 2)
    pass_on(0, 3)
    pass_on(1, 3)
    project_round(2)
    pass_on(2, 3)
    pass_on(3, 3)
    lax.fori_loop(0, 3, sum_first, 0)
    pass_on(0, 4)
    pass_on(2, 4)
    project_round(3)
    pass_on(1, 4)
    pass_on(3, 4)
    lax.fori_loop(3, 5, sum_first, 0)
    lax.fori_loop(0, 3, sum_second, 0)
    for p in range(CHUNKS):
        sib(p, 7, 4).wait_recv()
    project(7, 0)
    lax.fori_loop(5, 7, sum_first, 0)
    lax.fori_loop(3, 5, sum_second, 0)
    sum_first(7, 0)
    lax.fori_loop(5, 8, sum_second, 0)

    for n in range(8):
        un = b * 2 + n // 4
        mine = diagonal & (un == u) & (n % 4 == v)

        @pl.when(jnp.logical_not(mine))
        def _():
            remote(sum2.at[0], result.at[pl.ds(n * 16, 16)], last_send.at[0], last_recv.at[n], sibling).wait_recv()

    out_ref[...] = result[...].astype(jnp.float32).T.astype(jnp.bfloat16)

    @pl.when(jnp.logical_not(diagonal))
    def _():
        w_swap.wait_send()
        for p in range(CHUNKS):
            swap(p).wait_send()

    for n in range(NZ):
        for k in range(3):
            if n > 0 or k > 0:
                from_near(k, n).wait_send()
        for k in (0, 1):
            if n > 0 or k > 0:
                half(k, n).wait_send()
        if n > 0:
            from_far(n).wait_send()

    def drain(p, carry):
        sib(p, 0, 0).wait_send()
        sib(p, 7, 4).wait_send()
        for i in (0, 1):
            for s in (1, 2, 3):
                sib_of(p, i, s).wait_send()
            for s in (2, 3):
                ring(i, p, s).wait_send()

            ring(i, p, 1).wait_send()

            @pl.when((p < 2) if i == 0 else (p >= 2))
            def _():
                ring(i, p, 4).wait_send()

        return carry

    lax.fori_loop(0, CHUNKS, drain, 0)

    def drain_sums(n, carry):
        for j in (1, 2, 3):
            first_copy(n, j).wait_send()
            second_copy(n, j).wait_send()

        @pl.when(jnp.logical_not(stays(n)))
        def _():
            last_copy(n).wait_send()

        return carry

    lax.fori_loop(0, NZ, drain_sums, 0)


def per_device(queries, compressed, kv_up, w_out, positions, latent_gain):
    bf16, f32 = jnp.bfloat16, jnp.float32
    dma = pltpu.SemaphoreType.DMA
    any_space = pl.BlockSpec(memory_space=pl.ANY)
    vmem = pl.BlockSpec(memory_space=pltpu.VMEM)
    return pl.pallas_call(
        kernel,
        out_shape=jax.ShapeDtypeStruct((COLS, ROWS), bf16),
        in_specs=[any_space, vmem, any_space, any_space, vmem, vmem],
        out_specs=vmem,
        scratch_shapes=[
            pltpu.VMEM((NZ * 2 * ROWS, WIDE), bf16),
            pltpu.VMEM((HEADS_DEV, ROWS, 256), bf16),
            pltpu.VMEM((ROWS, HEADS_DEV * QK), bf16),
            pltpu.VMEM((LAT, HEADS_DEV * 256), bf16),
            pltpu.VMEM((HEADS_DEV, VD, LAT), bf16),
            pltpu.VMEM((HEADS_DEV, 8, ROWS), f32),
            pltpu.VMEM((HEADS_DEV, VD, ROWS), f32),
            pltpu.VMEM((CHUNKS, ROWS, 256), bf16),
            pltpu.VMEM((CHUNKS, NZ * 2 * ROWS, 256), bf16),
            pltpu.VMEM((COLS, HEADS_DEV * VD), bf16),
            pltpu.VMEM((NZ, 2 * ROWS, COLS), bf16),
            pltpu.VMEM((NZ, 3, 64, COLS), bf16),
            pltpu.VMEM((NZ, 64, COLS), bf16),
            pltpu.VMEM((NZ, 3, 16, COLS), bf16),
            pltpu.VMEM((NZ, 16, COLS), bf16),
            pltpu.VMEM((ROWS, COLS), bf16),
            dma((NZ,)), dma((NZ,)),
            dma((3, NZ)), dma((3, NZ)),
            dma((2, NZ)), dma((2, NZ)),
            dma, dma,
            dma((3,)),
            dma((2, CHUNKS, 4)), dma((2, CHUNKS, 4)),
            dma((CHUNKS, 8)), dma((CHUNKS, 8)),
            dma((CHUNKS,)), dma((CHUNKS,)),
            dma((NZ, 3)), dma((NZ, 3)),
            dma((NZ, 3)), dma((NZ, 3)),
            dma((NZ,)), dma((NZ,)),
        ],
        compiler_params=pltpu.CompilerParams(
            collective_id=0, has_side_effects=True, vmem_limit_bytes=56 * 1024 * 1024
        ),
        name="prefill",
    )(queries, compressed.T, kv_up, w_out.T, positions.reshape(1, ROWS), latent_gain.reshape(1, LAT)).T


def solution(mesh):
    in_specs = (P("ctx", "head"), P("ctx", None), P(None, "head"), P("head", "ctx"), P("ctx"), P())
    return jax.shard_map(
        per_device, mesh=mesh, in_specs=in_specs, out_specs=P("head", "ctx"), check_vma=False
    )
```

```python
import math

import jax
import jax.numpy as jnp
from jax import lax
from jax.experimental import pallas as pl
from jax.experimental.pallas import tpu as pltpu
from jax.sharding import PartitionSpec as P

LAT = 512
NOPE = 128
ROPE = 64
VD = 128
QK = 192
WIDE = 640
ROWS = 128
HEADS_DEV = 8
CHUNKS = 4
NZ = 8
COLS = 448
MESH = pl.DeviceIdType.MESH
SCALE = math.log2(math.e) / math.sqrt(QK)
NT = (((1,), (1,)), ((), ()))


def kernel(
    q_hbm, comp_ref, kv_hbm, w_hbm, pos_ref, gain_ref, out_ref,
    packed, qcat, q_in, kv_in, kv_t, stats, acc, att, full, w_both, part, got1, sum1, got2, sum2, result,
    far_send, far_recv, near_send, near_recv, half_send, half_recv,
    w_send, w_recv, w2_send, w2_recv, load_sem,
    ring_send, ring_recv, swap_send, swap_recv,
    first_send, first_recv, second_send, second_recv, last_send, last_recv,
):
    ctx, head = lax.axis_index("ctx"), lax.axis_index("head")
    z, a = ctx // 2, ctx % 2
    xh, y, b = head // 8, (head // 2) % 4, head % 2
    x = xh * 2 + a
    diagonal = a == b
    partner = (z * 2 + b, xh * 8 + y * 2 + a)
    sibling = (ctx, xh * 8 + y * 2 + (1 - b))

    def along_z(d):
        return (((z + d + NZ) % NZ) * 2 + a, head)

    def partner_z(d):
        return (((z + d + NZ) % NZ) * 2 + b, xh * 8 + y * 2 + a)

    def in_plane(px, py, core):
        return (z * 2 + px % 2, (px // 2) * 8 + py * 2 + core)

    def block(dz, core):
        return ((z + dz + 2 * NZ) % NZ) * 2 + core

    def rows(blk):
        return pl.ds(pl.multiple_of(blk * ROWS, ROWS), ROWS)

    def remote(src, dst, send, recv, device):
        return pltpu.make_async_remote_copy(
            src_ref=src, dst_ref=dst, send_sem=send, recv_sem=recv, device_id=device, device_id_type=MESH
        )

    kv_load = pltpu.make_async_copy(kv_hbm, kv_in, load_sem.at[0])
    q_load = pltpu.make_async_copy(q_hbm, q_in, load_sem.at[1])
    kv_load.start()
    q_load.start()

    bar = pltpu.get_barrier_semaphore()

    def greet(k, carry):
        pl.semaphore_signal(
            bar, inc=1, device_id=in_plane((x + k // 4) % 4, (y + k % 4) % 4, b), device_id_type=MESH
        )
        return carry

    lax.fori_loop(1, 16, greet, 0)
    pl.semaphore_signal(bar, inc=1, device_id=sibling, device_id_type=MESH)

    @pl.when(jnp.logical_not(diagonal))
    def _():
        pl.semaphore_signal(bar, inc=1, device_id=partner, device_id_type=MESH)

    for d in range(1, NZ):
        pl.semaphore_signal(bar, inc=1, device_id=along_z(d), device_id_type=MESH)
    for d in (1, -1):

        @pl.when(jnp.logical_not(diagonal))
        def _():
            pl.semaphore_signal(bar, inc=1, device_id=partner_z(d), device_id_type=MESH)

    latent = comp_ref[:LAT, :].astype(jnp.float32).T
    normed = latent * lax.rsqrt(jnp.mean(latent * latent, axis=-1, keepdims=True) + 1e-06) * gain_ref[...]
    own = rows(ctx)
    packed[own, :LAT] = normed.astype(jnp.bfloat16)
    pos = pos_ref[...]
    high = jnp.broadcast_to((pos >> 6).astype(jnp.float32), (ROWS, ROWS)).T
    low = jnp.broadcast_to((pos & 63).astype(jnp.float32), (ROWS, ROWS)).T
    lane = lax.broadcasted_iota(jnp.int32, (ROWS, ROWS), 1)
    rope = comp_ref[LAT:, :].astype(jnp.float32)
    rope = jnp.concatenate([rope, rope], axis=0).T
    tail = jnp.where(lane < 64, rope, jnp.where(lane < 96, high, low))
    packed[own, LAT:] = tail.astype(jnp.bfloat16)

    pl.semaphore_wait(bar, jnp.where(diagonal, 23, 26))

    def far(n):
        return (z + jnp.where(n % 2 == 1, -((n + 1) // 2), n // 2) + NZ) % NZ

    w_swap = remote(w_hbm, w_both.at[a], w_send, w_recv, partner)
    w_load = pltpu.make_async_copy(w_hbm, w_both.at[b], load_sem.at[2])
    w_share = remote(w_both.at[b], w_both.at[b], w2_send, w2_recv, sibling)

    def piece(n, col, first, count):
        start = (far(n) * 2 + col) * ROWS + b * 64 + first
        return packed.at[pl.ds(pl.multiple_of(start, 32), count)]

    def from_far(n):
        d = (n + 1) // 2 if n % 2 == 1 else -(n // 2)
        hop = n in (5, 6)
        if hop:
            d = 1 if n == 5 else -1
        ref = piece(n - 2 if hop else 0, a, (y % 2) * 32, 32)
        return remote(ref, ref, far_send.at[n], far_recv.at[n], along_z(d))

    def from_near(k, n):
        ref = piece(n, a, (y % 2) * 32, 32)
        turn = 1 - 2 * b
        device = in_plane((x + 4 + turn * (k > 0)) % 4, (y + 4 + turn * (k != 1)) % 4, b)
        return remote(ref, ref, near_send.at[k, n], near_recv.at[k, n], device)

    def half(k, n):
        ref = piece(n, 1 - a if k else a, 0, 64)
        return remote(ref, ref, half_send.at[k, n], half_recv.at[k, n], sibling)

    def go(copies):
        for copy in copies:
            copy.start()

    def arrive(copies):
        for copy in copies:
            copy.wait_recv()

    go([from_far(n) for n in (1, 2, 3, 4, 7)])
    go([from_near(1, 0), from_near(2, 0)])

    @pl.when(jnp.logical_not(diagonal))
    def _():
        w_swap.start()

    @pl.when(diagonal)
    def _():
        w_load.start()

    kv_load.wait()
    for h in range(HEADS_DEV):
        kv_t[h] = kv_in[:, h * 256 + NOPE : (h + 1) * 256].astype(jnp.float32).T.astype(jnp.bfloat16)
    q_load.wait()
    for j in range(HEADS_DEV // 2):
        first = q_in[:, j * 384 : j * 384 + 128]
        second = q_in[:, j * 384 + 128 : j * 384 + 256].astype(jnp.float32)
        third = q_in[:, j * 384 + 256 : j * 384 + 384].astype(jnp.float32)
        second_turned = pltpu.roll(second, 64, 1)
        third_turned = pltpu.roll(third, 64, 1)
        qcat[2 * j, :, :NOPE] = first
        qcat[2 * j, :, NOPE:] = jnp.where(lane < 64, second, 0.0).astype(jnp.bfloat16)
        qcat[2 * j + 1, :, :NOPE] = jnp.where(lane < 64, second_turned, third_turned).astype(jnp.bfloat16)
        qcat[2 * j + 1, :, NOPE:] = jnp.where(lane < 64, third_turned, 0.0).astype(jnp.bfloat16)

    for h in range(HEADS_DEV):
        stats[h, 0:1, :] = jnp.full((1, ROWS), -1e30, jnp.float32)
        stats[h, 1:2, :] = jnp.zeros((1, ROWS), jnp.float32)
        acc[h] = jnp.zeros((VD, ROWS), jnp.float32)

    def attend(blk0, blk1, pairs):
        both = jnp.concatenate([packed[rows(blk0), :LAT], packed[rows(blk1), :LAT]], axis=0)
        extra = jnp.concatenate([packed[rows(blk0), LAT:], packed[rows(blk1), LAT:]], axis=0)
        wide = extra.astype(jnp.float32)
        key_pos = wide[:, 64:65] * 64.0 + wide[:, 96:97]
        bias = jnp.where(key_pos <= pos.astype(jnp.float32), 0.0, -1e30)
        heads = [2 * hp + i for hp in pairs for i in (0, 1)]
        ks, vs = {}, {}
        for hp in pairs:
            k_cols = jnp.concatenate([kv_in[:, hp * 512 + i * 256 : hp * 512 + i * 256 + NOPE] for i in (0, 1)], axis=1)
            ks[hp] = jnp.dot(both, k_cols, preferred_element_type=jnp.float32).astype(jnp.bfloat16)
            v_rows = jnp.concatenate([kv_t[hp * 2], kv_t[hp * 2 + 1]], axis=0)
            vs[hp] = lax.dot_general(v_rows, both, NT, preferred_element_type=jnp.float32).astype(jnp.bfloat16)
        scores, exps, fades = {}, {}, {}
        for h in heads:
            k_all = jnp.concatenate([ks[h // 2][:, h % 2 * 128 : h % 2 * 128 + 128], extra], axis=1)
            scores[h] = lax.dot_general(k_all, qcat[h], NT, preferred_element_type=jnp.float32) * SCALE + bias
        for h in heads:
            before = stats[h, 0:1, :]
            top = jnp.maximum(before, jnp.max(scores[h], axis=0, keepdims=True))
            fade = jnp.exp2(before - top)
            e = jnp.exp2(scores[h] - top)
            stats[h, 0:1, :] = top
            stats[h, 1:2, :] = stats[h, 1:2, :] * fade + jnp.sum(e, axis=0, keepdims=True)
            exps[h] = e.astype(jnp.bfloat16)
            fades[h] = fade
        for h in heads:
            v = vs[h // 2][h % 2 * 128 : h % 2 * 128 + 128, :]
            acc[h] = acc[h] * fades[h] + jnp.dot(v, exps[h], preferred_element_type=jnp.float32)

    def from_z(*ns):
        for n in ns:
            from_far(n).wait_recv()
            if n in (3, 4):
                from_far(n + 2).start()
            go([from_near(k, n) for k in range(3)])

    def from_plane(*ns):
        for n in ns:
            arrive([from_near(k, n) for k in range(3)])
            go([half(k, n) for k in (0, 1)])

    def before_stage(g):
        if g == 0:
            arrive([from_near(1, 0), from_near(2, 0)])
            half(1, 0).start()
            from_z(1, 2)
            half(1, 0).wait_recv()
        if g == 1:
            from_z(3, 4)
            from_plane(1, 2)
        if g == 2:
            from_z(5, 6)
        if g == 3:
            from_z(7)
            from_plane(3, 4)
        if g == 4:
            from_plane(5)
        if g == 5:
            from_plane(6)
        if g == 6:
            from_plane(7)
        if g > 0:
            arrive([half(k, g) for k in (0, 1)])

    def stage(g, carry):
        for k in range(NZ - 1):
            @pl.when(g == k)
            def _():
                before_stage(k)

        attend(far(g) * 2, far(g) * 2 + 1, range(HEADS_DEV // 2))
        return carry

    lax.fori_loop(0, NZ - 1, stage, 0)
    before_stage(NZ - 1)

    def ring(i, p, s):
        d = 1 if i == 0 else -1
        r = rows(block(-d * (s - 1), b))
        return remote(full.at[p, r], full.at[p, r], ring_send.at[i, p, s - 1], ring_recv.at[i, p, s - 1], along_z(d))

    def swap(p):
        return remote(att.at[p], full.at[p, own], swap_send.at[p], swap_recv.at[p], partner)

    def ring_first(i, p):
        return remote(
            att.at[p], full.at[p, own], ring_send.at[i, p, 0], ring_recv.at[i, p, 0], partner_z(1 if i == 0 else -1)
        )

    def pass_on(p, s):
        if s < 4:
            for i in (0, 1):
                ring(i, p, s).wait_recv()
                if s < 3 or i == p // 2:
                    ring(i, p, s + 1).start()
        else:
            ring(p // 2, p, 4).wait_recv()

    for p in range(CHUNKS):
        if p % 2 == 0:
            attend(far(NZ - 1) * 2, far(NZ - 1) * 2 + 1, (p, p + 1))
        for i in (0, 1):
            o = acc[2 * p + i] / stats[2 * p + i, 1:2, :]
            att[p, :, i * VD : (i + 1) * VD] = o.T.astype(jnp.bfloat16)
        ring_first(0, p).start()
        ring_first(1, p).start()

        @pl.when(diagonal)
        def _():
            full[p, own, :] = att[p]

        @pl.when(jnp.logical_not(diagonal))
        def _():
            swap(p).start()

    @pl.when(diagonal)
    def _():
        w_load.wait()

    @pl.when(jnp.logical_not(diagonal))
    def _():
        w_swap.wait_recv()

    w_share.start()
    pass_on(0, 1)
    pass_on(1, 1)

    @pl.when(jnp.logical_not(diagonal))
    def _():
        for p in range(CHUNKS):
            swap(p).wait_recv()

    u = jnp.where(b == 0, y, x)
    v = jnp.where(b == 0, x, y)

    def first_copy(n, j):
        t = (u + j) % 4
        device = in_plane(jnp.where(b == 0, x, t), jnp.where(b == 0, t, y), b)
        src = part.at[n, pl.ds(pl.multiple_of(t * 64, 64), 64)]
        return remote(src, got1.at[n, j - 1], first_send.at[n, j - 1], first_recv.at[n, j - 1], device)

    def second_copy(n, j):
        t = (v + j) % 4
        device = in_plane(jnp.where(b == 0, t, x), jnp.where(b == 0, y, t), b)
        src = sum1.at[n, pl.ds(pl.multiple_of(t * 16, 16), 16)]
        return remote(src, got2.at[n, j - 1], second_send.at[n, j - 1], second_recv.at[n, j - 1], device)

    def project(n, carry):
        r = rows(far(n) * 2 + b)
        lhs = jnp.concatenate([full[p, r, :] for p in range(CHUNKS)], axis=1)
        for i in (0, 1):
            part[n, i * ROWS : (i + 1) * ROWS, :] = lax.dot_general(
                lhs, w_both[i], NT, preferred_element_type=jnp.float32
            ).astype(jnp.bfloat16)
        for j in (1, 2, 3):
            first_copy(n, j).start()
        return carry

    def sum_first(n, carry):
        total = part[n, pl.ds(pl.multiple_of(u * 64, 64), 64), :].astype(jnp.float32)
        for j in (1, 2, 3):
            first_copy(n, j).wait_recv()
        for j in (1, 2, 3):
            total = total + got1[n, j - 1].astype(jnp.float32)
        sum1[n] = total.astype(jnp.bfloat16)
        for j in (1, 2, 3):
            second_copy(n, j).start()
        return carry

    slot = (u % 2) * 4 + v

    def last_copy(n):
        zp = far(n)
        device = in_plane((zp // 4) * 2 + u // 2, zp % 4, b)
        return remote(
            sum2.at[n], result.at[pl.ds(pl.multiple_of(slot * 16, 16), 16)], last_send.at[n], last_recv.at[slot], device
        )

    def stays(n):
        zp = far(n)
        return (u // 2 == a) & (zp == xh * 4 + y)

    def sum_second(n, carry):
        total = sum1[n, pl.ds(pl.multiple_of(v * 16, 16), 16), :].astype(jnp.float32)
        for j in (1, 2, 3):
            second_copy(n, j).wait_recv()
        for j in (1, 2, 3):
            total = total + got2[n, j - 1].astype(jnp.float32)
        sum2[n] = total.astype(jnp.bfloat16)

        @pl.when(stays(n))
        def _():
            result[pl.ds(pl.multiple_of(slot * 16, 16), 16), :] = sum2[n]

        @pl.when(jnp.logical_not(stays(n)))
        def _():
            last_copy(n).start()

        return carry

    def project_round(s):
        lax.fori_loop(2 * s - 1, 2 * s + 1, project, 0)

    for p in (2, 3):
        pass_on(p, 1)
    w_share.wait_recv()
    project(0, 0)

    for n in range(NZ):
        for k in range(3):
            if n > 0 or k > 0:
                from_near(k, n).wait_send()
        for k in (0, 1):
            if n > 0 or k > 0:
                half(k, n).wait_send()
        if n > 0:
            from_far(n).wait_send()

    @pl.when(jnp.logical_not(diagonal))
    def _():
        w_swap.wait_send()
        for p in range(CHUNKS):
            swap(p).wait_send()

    pass_on(0, 2)
    pass_on(1, 2)
    project_round(1)
    pass_on(2, 2)
    pass_on(3, 2)
    pass_on(0, 3)
    pass_on(1, 3)
    project_round(2)
    pass_on(2, 3)
    pass_on(3, 3)
    lax.fori_loop(0, 3, sum_first, 0)
    pass_on(0, 4)
    pass_on(2, 4)
    project_round(3)
    pass_on(1, 4)
    pass_on(3, 4)
    lax.fori_loop(3, 5, sum_first, 0)
    lax.fori_loop(0, 3, sum_second, 0)
    project(7, 0)
    w_share.wait_send()
    for p in range(CHUNKS):
        for i in (0, 1):
            for s in (1, 2, 3):
                ring(i, p, s).wait_send()
        ring(p // 2, p, 4).wait_send()
    lax.fori_loop(5, 7, sum_first, 0)
    lax.fori_loop(3, 5, sum_second, 0)
    sum_first(7, 0)

    def first_left(n, carry):
        for j in (1, 2, 3):
            first_copy(n, j).wait_send()
        return carry

    def second_left(n, carry):
        for j in (1, 2, 3):
            second_copy(n, j).wait_send()
        return carry

    lax.fori_loop(0, NZ, first_left, 0)
    lax.fori_loop(5, 8, sum_second, 0)
    lax.fori_loop(0, NZ, second_left, 0)

    for n in range(8):
        un = a * 2 + n // 4
        mine = (un == u) & (n % 4 == v)

        @pl.when(jnp.logical_not(mine))
        def _():
            remote(sum2.at[0], result.at[pl.ds(n * 16, 16)], last_send.at[0], last_recv.at[n], sibling).wait_recv()

    out_ref[...] = result[...].astype(jnp.float32).T.astype(jnp.bfloat16)

    for n in range(NZ):
        @pl.when(jnp.logical_not(stays(n)))
        def _():
            last_copy(n).wait_send()


def per_device(queries, compressed, kv_up, w_out, positions, latent_gain):
    bf16, f32 = jnp.bfloat16, jnp.float32
    dma = pltpu.SemaphoreType.DMA
    any_space = pl.BlockSpec(memory_space=pl.ANY)
    vmem = pl.BlockSpec(memory_space=pltpu.VMEM)
    return pl.pallas_call(
        kernel,
        out_shape=jax.ShapeDtypeStruct((COLS, ROWS), bf16),
        in_specs=[any_space, vmem, any_space, any_space, vmem, vmem],
        out_specs=vmem,
        scratch_shapes=[
            pltpu.VMEM((NZ * 2 * ROWS, WIDE), bf16),
            pltpu.VMEM((HEADS_DEV, ROWS, 256), bf16),
            pltpu.VMEM((ROWS, HEADS_DEV * QK), bf16),
            pltpu.VMEM((LAT, HEADS_DEV * 256), bf16),
            pltpu.VMEM((HEADS_DEV, VD, LAT), bf16),
            pltpu.VMEM((HEADS_DEV, 8, ROWS), f32),
            pltpu.VMEM((HEADS_DEV, VD, ROWS), f32),
            pltpu.VMEM((CHUNKS, ROWS, 256), bf16),
            pltpu.VMEM((CHUNKS, NZ * 2 * ROWS, 256), bf16),
            pltpu.VMEM((2, COLS, HEADS_DEV * VD), bf16),
            pltpu.VMEM((NZ, 2 * ROWS, COLS), bf16),
            pltpu.VMEM((NZ, 3, 64, COLS), bf16),
            pltpu.VMEM((NZ, 64, COLS), bf16),
            pltpu.VMEM((NZ, 3, 16, COLS), bf16),
            pltpu.VMEM((NZ, 16, COLS), bf16),
            pltpu.VMEM((ROWS, COLS), bf16),
            dma((NZ,)), dma((NZ,)),
            dma((3, NZ)), dma((3, NZ)),
            dma((2, NZ)), dma((2, NZ)),
            dma, dma,
            dma, dma,
            dma((3,)),
            dma((2, CHUNKS, 4)), dma((2, CHUNKS, 4)),
            dma((CHUNKS,)), dma((CHUNKS,)),
            dma((NZ, 3)), dma((NZ, 3)),
            dma((NZ, 3)), dma((NZ, 3)),
            dma((NZ,)), dma((NZ,)),
        ],
        compiler_params=pltpu.CompilerParams(
            collective_id=0, has_side_effects=True, vmem_limit_bytes=56 * 1024 * 1024
        ),
        name="prefill",
    )(queries, compressed.T, kv_up, w_out.T, positions.reshape(1, ROWS), latent_gain.reshape(1, LAT)).T


def solution(mesh):
    in_specs = (P("ctx", "head"), P("ctx", None), P(None, "head"), P("head", "ctx"), P("ctx"), P())
    return jax.shard_map(
        per_device, mesh=mesh, in_specs=in_specs, out_specs=P("head", "ctx"), check_vma=False
    )
```

```python
import math

import jax
import jax.numpy as jnp
from jax import lax
from jax.experimental import pallas as pl
from jax.experimental.pallas import tpu as pltpu
from jax.sharding import PartitionSpec as P

LAT = 512
NOPE = 128
ROPE = 64
VD = 128
QK = 192
WIDE = 640
ROWS = 128
HEADS_DEV = 8
CHUNKS = 4
NZ = 8
COLS = 448
MESH = pl.DeviceIdType.MESH
SCALE = math.log2(math.e) / math.sqrt(QK)
NT = (((1,), (1,)), ((), ()))


def kernel(
    q_hbm, comp_hbm, kv_hbm, w_hbm, pos_hbm, gain_hbm, out_ref,
    comp_ref, pos_ref, gain_ref, packed, qcat, q_in, kv_in, kv_t, stats, acc, att, full, w_both, part, got1, sum1, got2, sum2, result,
    far_send, far_recv, near_send, near_recv, half_send, half_recv,
    w_send, w_recv, w2_send, w2_recv, load_sem,
    ring_send, ring_recv, swap_send, swap_recv,
    first_send, first_recv, second_send, second_recv, last_send, last_recv,
):
    ctx, head = lax.axis_index("ctx"), lax.axis_index("head")
    z, a = ctx // 2, ctx % 2
    xh, y, b = head // 8, (head // 2) % 4, head % 2
    x = xh * 2 + a
    diagonal = a == b
    partner = (z * 2 + b, xh * 8 + y * 2 + a)
    sibling = (ctx, xh * 8 + y * 2 + (1 - b))

    def along_z(d):
        return (((z + d + NZ) % NZ) * 2 + a, head)

    def partner_z(d):
        return (((z + d + NZ) % NZ) * 2 + b, xh * 8 + y * 2 + a)

    def in_plane(px, py, core):
        return (z * 2 + px % 2, (px // 2) * 8 + py * 2 + core)

    def block(dz, core):
        return ((z + dz + 2 * NZ) % NZ) * 2 + core

    def rows(blk):
        return pl.ds(pl.multiple_of(blk * ROWS, ROWS), ROWS)

    def remote(src, dst, send, recv, device):
        return pltpu.make_async_remote_copy(
            src_ref=src, dst_ref=dst, send_sem=send, recv_sem=recv, device_id=device, device_id_type=MESH
        )

    kv_load = pltpu.make_async_copy(kv_hbm, kv_in, load_sem.at[0])
    q_load = pltpu.make_async_copy(q_hbm, q_in, load_sem.at[1])
    small = [
        pltpu.make_async_copy(src, dst, load_sem.at[3 + i])
        for i, (src, dst) in enumerate([(comp_hbm, comp_ref), (pos_hbm, pos_ref), (gain_hbm, gain_ref)])
    ]
    for load in small:
        load.start()
    kv_load.start()
    q_load.start()

    bar = pltpu.get_barrier_semaphore()

    def greet(k, carry):
        pl.semaphore_signal(
            bar, inc=1, device_id=in_plane((x + k // 4) % 4, (y + k % 4) % 4, b), device_id_type=MESH
        )
        return carry

    for d in range(1, NZ):
        pl.semaphore_signal(bar, inc=1, device_id=along_z(d), device_id_type=MESH)
    for d in (1, -1):

        @pl.when(jnp.logical_not(diagonal))
        def _():
            pl.semaphore_signal(bar, inc=1, device_id=partner_z(d), device_id_type=MESH)

    lax.fori_loop(1, 16, greet, 0)
    pl.semaphore_signal(bar, inc=1, device_id=sibling, device_id_type=MESH)

    @pl.when(jnp.logical_not(diagonal))
    def _():
        pl.semaphore_signal(bar, inc=1, device_id=partner, device_id_type=MESH)

    for load in small:
        load.wait()

    latent = comp_ref[:LAT, :].astype(jnp.float32).T
    normed = latent * lax.rsqrt(jnp.mean(latent * latent, axis=-1, keepdims=True) + 1e-06) * gain_ref[...]
    own = rows(ctx)
    packed[own, :LAT] = normed.astype(jnp.bfloat16)
    pos = pos_ref[...]
    high = jnp.broadcast_to((pos >> 6).astype(jnp.float32), (ROWS, ROWS)).T
    low = jnp.broadcast_to((pos & 63).astype(jnp.float32), (ROWS, ROWS)).T
    lane = lax.broadcasted_iota(jnp.int32, (ROWS, ROWS), 1)
    rope = comp_ref[LAT:, :].astype(jnp.float32)
    rope = jnp.concatenate([rope, rope], axis=0).T
    tail = jnp.where(lane < 64, rope, jnp.where(lane < 96, high, low))
    packed[own, LAT:] = tail.astype(jnp.bfloat16)

    pl.semaphore_wait(bar, jnp.where(diagonal, 23, 26))

    def far(n):
        return (z + jnp.where(n % 2 == 1, -((n + 1) // 2), n // 2) + NZ) % NZ

    w_swap = remote(w_hbm, w_both.at[a], w_send, w_recv, partner)
    w_load = pltpu.make_async_copy(w_hbm, w_both.at[b], load_sem.at[2])
    w_share = remote(w_both.at[b], w_both.at[b], w2_send, w2_recv, sibling)

    def piece(n, col, first, count):
        start = (far(n) * 2 + col) * ROWS + b * 64 + first
        return packed.at[pl.ds(pl.multiple_of(start, 32), count)]

    def from_far(n):
        d = (n + 1) // 2 if n % 2 == 1 else -(n // 2)
        hop = n in (5, 6)
        if hop:
            d = 1 if n == 5 else -1
        ref = piece(n - 2 if hop else 0, a, (y % 2) * 32, 32)
        return remote(ref, ref, far_send.at[n], far_recv.at[n], along_z(d))

    def from_near(k, n):
        ref = piece(n, a, (y % 2) * 32, 32)
        turn = 1 - 2 * b
        device = in_plane((x + 4 + turn * (k > 0)) % 4, (y + 4 + turn * (k != 1)) % 4, b)
        return remote(ref, ref, near_send.at[k, n], near_recv.at[k, n], device)

    def half(k, n):
        ref = piece(n, 1 - a if k else a, 0, 64)
        return remote(ref, ref, half_send.at[k, n], half_recv.at[k, n], sibling)

    def go(copies):
        for copy in copies:
            copy.start()

    def arrive(copies):
        for copy in copies:
            copy.wait_recv()

    go([from_far(n) for n in (1, 2, 3, 4, 7)])
    go([from_near(1, 0), from_near(2, 0)])

    @pl.when(jnp.logical_not(diagonal))
    def _():
        w_swap.start()

    @pl.when(diagonal)
    def _():
        w_load.start()

    kv_load.wait()
    for h in range(HEADS_DEV):
        kv_t[h] = kv_in[:, h * 256 + NOPE : (h + 1) * 256].astype(jnp.float32).T.astype(jnp.bfloat16)
    q_load.wait()
    for j in range(HEADS_DEV // 2):
        first = q_in[:, j * 384 : j * 384 + 128]
        second = q_in[:, j * 384 + 128 : j * 384 + 256].astype(jnp.float32)
        third = q_in[:, j * 384 + 256 : j * 384 + 384].astype(jnp.float32)
        second_turned = pltpu.roll(second, 64, 1)
        third_turned = pltpu.roll(third, 64, 1)
        qcat[2 * j, :, :NOPE] = first
        qcat[2 * j, :, NOPE:] = jnp.where(lane < 64, second, 0.0).astype(jnp.bfloat16)
        qcat[2 * j + 1, :, :NOPE] = jnp.where(lane < 64, second_turned, third_turned).astype(jnp.bfloat16)
        qcat[2 * j + 1, :, NOPE:] = jnp.where(lane < 64, third_turned, 0.0).astype(jnp.bfloat16)

    for h in range(HEADS_DEV):
        stats[h, 0:1, :] = jnp.full((1, ROWS), -1e30, jnp.float32)
        stats[h, 1:2, :] = jnp.zeros((1, ROWS), jnp.float32)
        acc[h] = jnp.zeros((VD, ROWS), jnp.float32)

    def attend(blk0, blk1, pairs):
        both = jnp.concatenate([packed[rows(blk0), :LAT], packed[rows(blk1), :LAT]], axis=0)
        extra = jnp.concatenate([packed[rows(blk0), LAT:], packed[rows(blk1), LAT:]], axis=0)
        wide = extra.astype(jnp.float32)
        key_pos = wide[:, 64:65] * 64.0 + wide[:, 96:97]
        bias = jnp.where(key_pos <= pos.astype(jnp.float32), 0.0, -1e30)
        heads = [2 * hp + i for hp in pairs for i in (0, 1)]
        ks, vs = {}, {}
        for hp in pairs:
            k_cols = jnp.concatenate([kv_in[:, hp * 512 + i * 256 : hp * 512 + i * 256 + NOPE] for i in (0, 1)], axis=1)
            ks[hp] = jnp.dot(both, k_cols, preferred_element_type=jnp.float32).astype(jnp.bfloat16)
            v_rows = jnp.concatenate([kv_t[hp * 2], kv_t[hp * 2 + 1]], axis=0)
            vs[hp] = lax.dot_general(v_rows, both, NT, preferred_element_type=jnp.float32).astype(jnp.bfloat16)
        scores, exps, fades = {}, {}, {}
        for h in heads:
            k_all = jnp.concatenate([ks[h // 2][:, h % 2 * 128 : h % 2 * 128 + 128], extra], axis=1)
            scores[h] = lax.dot_general(k_all, qcat[h], NT, preferred_element_type=jnp.float32) * SCALE + bias
        for h in heads:
            before = stats[h, 0:1, :]
            top = jnp.maximum(before, jnp.max(scores[h], axis=0, keepdims=True))
            fade = jnp.exp2(before - top)
            e = jnp.exp2(scores[h] - top)
            stats[h, 0:1, :] = top
            stats[h, 1:2, :] = stats[h, 1:2, :] * fade + jnp.sum(e, axis=0, keepdims=True)
            exps[h] = e.astype(jnp.bfloat16)
            fades[h] = fade
        for h in heads:
            v = vs[h // 2][h % 2 * 128 : h % 2 * 128 + 128, :]
            acc[h] = acc[h] * fades[h] + jnp.dot(v, exps[h], preferred_element_type=jnp.float32)

    def from_z(*ns):
        for n in ns:
            from_far(n).wait_recv()
            if n in (3, 4):
                from_far(n + 2).start()
            go([from_near(k, n) for k in range(3)])

    def from_plane(*ns):
        for n in ns:
            arrive([from_near(k, n) for k in range(3)])
            go([half(k, n) for k in (0, 1)])

    def before_stage(g):
        if g == 0:
            arrive([from_near(1, 0), from_near(2, 0)])
            half(1, 0).start()
            from_z(1, 2)
            half(1, 0).wait_recv()
        if g == 1:
            from_z(3, 4)
            from_plane(1, 2)
        if g == 2:
            from_z(5, 6)
        if g == 3:
            from_z(7)
            from_plane(3, 4)
        if g == 4:
            from_plane(5)
        if g == 5:
            from_plane(6)
        if g == 6:
            from_plane(7)
        if g > 0:
            arrive([half(k, g) for k in (0, 1)])

    def stage(g, carry):
        for k in range(NZ - 1):
            @pl.when(g == k)
            def _():
                before_stage(k)

        attend(far(g) * 2, far(g) * 2 + 1, range(HEADS_DEV // 2))
        return carry

    lax.fori_loop(0, NZ - 1, stage, 0)
    before_stage(NZ - 1)

    def ring(i, p, s):
        d = 1 if i == 0 else -1
        r = rows(block(-d * (s - 1), b))
        return remote(full.at[p, r], full.at[p, r], ring_send.at[i, p, s - 1], ring_recv.at[i, p, s - 1], along_z(d))

    def swap(p):
        return remote(att.at[p], full.at[p, own], swap_send.at[p], swap_recv.at[p], partner)

    def ring_first(i, p):
        return remote(
            att.at[p], full.at[p, own], ring_send.at[i, p, 0], ring_recv.at[i, p, 0], partner_z(1 if i == 0 else -1)
        )

    def pass_on(p, s):
        if s < 4:
            for i in (0, 1):
                ring(i, p, s).wait_recv()
                if s < 3 or i == p // 2:
                    ring(i, p, s + 1).start()
        else:
            ring(p // 2, p, 4).wait_recv()

    for p in range(CHUNKS):
        if p % 2 == 0:
            attend(far(NZ - 1) * 2, far(NZ - 1) * 2 + 1, (p, p + 1))
        for i in (0, 1):
            o = acc[2 * p + i] / stats[2 * p + i, 1:2, :]
            att[p, :, i * VD : (i + 1) * VD] = o.T.astype(jnp.bfloat16)
        ring_first(0, p).start()
        ring_first(1, p).start()

        @pl.when(diagonal)
        def _():
            full[p, own, :] = att[p]

        @pl.when(jnp.logical_not(diagonal))
        def _():
            swap(p).start()

    @pl.when(diagonal)
    def _():
        w_load.wait()

    @pl.when(jnp.logical_not(diagonal))
    def _():
        w_swap.wait_recv()

    w_share.start()
    pass_on(0, 1)
    pass_on(1, 1)

    @pl.when(jnp.logical_not(diagonal))
    def _():
        for p in range(CHUNKS):
            swap(p).wait_recv()

    u = jnp.where(b == 0, y, x)
    v = jnp.where(b == 0, x, y)

    def first_copy(n, j):
        t = (u + j) % 4
        device = in_plane(jnp.where(b == 0, x, t), jnp.where(b == 0, t, y), b)
        src = part.at[n, pl.ds(pl.multiple_of(t * 64, 64), 64)]
        return remote(src, got1.at[n, j - 1], first_send.at[n, j - 1], first_recv.at[n, j - 1], device)

    def second_copy(n, j):
        t = (v + j) % 4
        device = in_plane(jnp.where(b == 0, t, x), jnp.where(b == 0, y, t), b)
        src = sum1.at[n, pl.ds(pl.multiple_of(t * 16, 16), 16)]
        return remote(src, got2.at[n, j - 1], second_send.at[n, j - 1], second_recv.at[n, j - 1], device)

    def project(n, carry):
        r = rows(far(n) * 2 + b)
        lhs = jnp.concatenate([full[p, r, :] for p in range(CHUNKS)], axis=1)
        for i in (0, 1):
            part[n, i * ROWS : (i + 1) * ROWS, :] = lax.dot_general(
                lhs, w_both[i], NT, preferred_element_type=jnp.float32
            ).astype(jnp.bfloat16)
        for j in (1, 2, 3):
            first_copy(n, j).start()
        return carry

    def sum_first(n, carry):
        total = part[n, pl.ds(pl.multiple_of(u * 64, 64), 64), :].astype(jnp.float32)
        for j in (1, 2, 3):
            first_copy(n, j).wait_recv()
        for j in (1, 2, 3):
            total = total + got1[n, j - 1].astype(jnp.float32)
        sum1[n] = total.astype(jnp.bfloat16)
        for j in (1, 2, 3):
            second_copy(n, j).start()
        return carry

    slot = (u % 2) * 4 + v

    def last_copy(n):
        zp = far(n)
        device = in_plane((zp // 4) * 2 + u // 2, zp % 4, b)
        return remote(
            sum2.at[n], result.at[pl.ds(pl.multiple_of(slot * 16, 16), 16)], last_send.at[n], last_recv.at[slot], device
        )

    def stays(n):
        zp = far(n)
        return (u // 2 == a) & (zp == xh * 4 + y)

    def sum_second(n, carry):
        total = sum1[n, pl.ds(pl.multiple_of(v * 16, 16), 16), :].astype(jnp.float32)
        for j in (1, 2, 3):
            second_copy(n, j).wait_recv()
        for j in (1, 2, 3):
            total = total + got2[n, j - 1].astype(jnp.float32)
        sum2[n] = total.astype(jnp.bfloat16)

        @pl.when(stays(n))
        def _():
            result[pl.ds(pl.multiple_of(slot * 16, 16), 16), :] = sum2[n]

        @pl.when(jnp.logical_not(stays(n)))
        def _():
            last_copy(n).start()

        return carry

    def project_round(s):
        lax.fori_loop(2 * s - 1, 2 * s + 1, project, 0)

    for p in (2, 3):
        pass_on(p, 1)
    w_share.wait_recv()
    project(0, 0)

    for n in range(NZ):
        for k in range(3):
            if n > 0 or k > 0:
                from_near(k, n).wait_send()
        for k in (0, 1):
            if n > 0 or k > 0:
                half(k, n).wait_send()
        if n > 0:
            from_far(n).wait_send()

    @pl.when(jnp.logical_not(diagonal))
    def _():
        w_swap.wait_send()
        for p in range(CHUNKS):
            swap(p).wait_send()

    pass_on(0, 2)
    pass_on(1, 2)
    project_round(1)
    pass_on(2, 2)
    pass_on(3, 2)
    pass_on(0, 3)
    pass_on(1, 3)
    project_round(2)
    pass_on(2, 3)
    pass_on(3, 3)
    lax.fori_loop(0, 3, sum_first, 0)
    pass_on(0, 4)
    pass_on(2, 4)
    project_round(3)
    pass_on(1, 4)
    pass_on(3, 4)
    lax.fori_loop(3, 5, sum_first, 0)
    lax.fori_loop(0, 3, sum_second, 0)
    project(7, 0)
    w_share.wait_send()
    for p in range(CHUNKS):
        for i in (0, 1):
            for s in (1, 2, 3):
                ring(i, p, s).wait_send()
        ring(p // 2, p, 4).wait_send()
    lax.fori_loop(5, 7, sum_first, 0)
    lax.fori_loop(3, 5, sum_second, 0)
    sum_first(7, 0)

    def first_left(n, carry):
        for j in (1, 2, 3):
            first_copy(n, j).wait_send()
        return carry

    def second_left(n, carry):
        for j in (1, 2, 3):
            second_copy(n, j).wait_send()
        return carry

    lax.fori_loop(0, NZ, first_left, 0)
    lax.fori_loop(5, 8, sum_second, 0)
    lax.fori_loop(0, NZ, second_left, 0)

    for n in range(8):
        un = a * 2 + n // 4
        mine = (un == u) & (n % 4 == v)

        @pl.when(jnp.logical_not(mine))
        def _():
            remote(sum2.at[0], result.at[pl.ds(n * 16, 16)], last_send.at[0], last_recv.at[n], sibling).wait_recv()

    out_ref[...] = result[...].astype(jnp.float32).T.astype(jnp.bfloat16)

    for n in range(NZ):
        @pl.when(jnp.logical_not(stays(n)))
        def _():
            last_copy(n).wait_send()


def per_device(queries, compressed, kv_up, w_out, positions, latent_gain):
    bf16, f32 = jnp.bfloat16, jnp.float32
    dma = pltpu.SemaphoreType.DMA
    any_space = pl.BlockSpec(memory_space=pl.ANY)
    vmem = pl.BlockSpec(memory_space=pltpu.VMEM)
    return pl.pallas_call(
        kernel,
        out_shape=jax.ShapeDtypeStruct((COLS, ROWS), bf16),
        in_specs=[any_space] * 6,
        out_specs=vmem,
        scratch_shapes=[
            pltpu.VMEM((LAT + ROPE, ROWS), bf16),
            pltpu.VMEM((1, ROWS), jnp.int32),
            pltpu.VMEM((1, LAT), f32),
            pltpu.VMEM((NZ * 2 * ROWS, WIDE), bf16),
            pltpu.VMEM((HEADS_DEV, ROWS, 256), bf16),
            pltpu.VMEM((ROWS, HEADS_DEV * QK), bf16),
            pltpu.VMEM((LAT, HEADS_DEV * 256), bf16),
            pltpu.VMEM((HEADS_DEV, VD, LAT), bf16),
            pltpu.VMEM((HEADS_DEV, 8, ROWS), f32),
            pltpu.VMEM((HEADS_DEV, VD, ROWS), f32),
            pltpu.VMEM((CHUNKS, ROWS, 256), bf16),
            pltpu.VMEM((CHUNKS, NZ * 2 * ROWS, 256), bf16),
            pltpu.VMEM((2, COLS, HEADS_DEV * VD), bf16),
            pltpu.VMEM((NZ, 2 * ROWS, COLS), bf16),
            pltpu.VMEM((NZ, 3, 64, COLS), bf16),
            pltpu.VMEM((NZ, 64, COLS), bf16),
            pltpu.VMEM((NZ, 3, 16, COLS), bf16),
            pltpu.VMEM((NZ, 16, COLS), bf16),
            pltpu.VMEM((ROWS, COLS), bf16),
            dma((NZ,)), dma((NZ,)),
            dma((3, NZ)), dma((3, NZ)),
            dma((2, NZ)), dma((2, NZ)),
            dma, dma,
            dma, dma,
            dma((6,)),
            dma((2, CHUNKS, 4)), dma((2, CHUNKS, 4)),
            dma((CHUNKS,)), dma((CHUNKS,)),
            dma((NZ, 3)), dma((NZ, 3)),
            dma((NZ, 3)), dma((NZ, 3)),
            dma((NZ,)), dma((NZ,)),
        ],
        compiler_params=pltpu.CompilerParams(
            collective_id=0, has_side_effects=True, vmem_limit_bytes=56 * 1024 * 1024
        ),
        name="prefill",
    )(queries, compressed.T, kv_up, w_out.T, positions.reshape(1, ROWS), latent_gain.reshape(1, LAT)).T


def solution(mesh):
    in_specs = (P("ctx", "head"), P("ctx", None), P(None, "head"), P("head", "ctx"), P("ctx"), P())
    return jax.shard_map(
        per_device, mesh=mesh, in_specs=in_specs, out_specs=P("head", "ctx"), check_vma=False
    )
```

```python
import math

import jax
import jax.numpy as jnp
from jax import lax
from jax.experimental import pallas as pl
from jax.experimental.pallas import tpu as pltpu
from jax.sharding import PartitionSpec as P

LAT = 512
NOPE = 128
ROPE = 64
VD = 128
QK = 192
WIDE = 640
ROWS = 128
HEADS_DEV = 8
CHUNKS = 4
NZ = 8
COLS = 448
MESH = pl.DeviceIdType.MESH
SCALE = math.log2(math.e) / math.sqrt(QK)
NT = (((1,), (1,)), ((), ()))


def kernel(
    q_hbm, comp_hbm, kv_hbm, w_hbm, pos_hbm, gain_hbm, out_ref,
    comp_ref, pos_ref, gain_ref, packed, qcat, q_in, kv_in, kv_t, stats, acc, att, full, w_both, part, got1, sum1, got2, sum2, result,
    far_send, far_recv, near_send, near_recv, half_send, half_recv,
    w_send, w_recv, w2_send, w2_recv, load_sem,
    ring_send, ring_recv, swap_send, swap_recv,
    first_send, first_recv, second_send, second_recv, last_send, last_recv,
):
    ctx, head = lax.axis_index("ctx"), lax.axis_index("head")
    z, a = ctx // 2, ctx % 2
    xh, y, b = head // 8, (head // 2) % 4, head % 2
    x = xh * 2 + a
    diagonal = a == b
    partner = (z * 2 + b, xh * 8 + y * 2 + a)
    sibling = (ctx, xh * 8 + y * 2 + (1 - b))

    def along_z(d):
        return (((z + d + NZ) % NZ) * 2 + a, head)

    def partner_z(d):
        return (((z + d + NZ) % NZ) * 2 + b, xh * 8 + y * 2 + a)

    def in_plane(px, py, core):
        return (z * 2 + px % 2, (px // 2) * 8 + py * 2 + core)

    def block(dz, core):
        return ((z + dz + 2 * NZ) % NZ) * 2 + core

    def rows(blk):
        return pl.ds(pl.multiple_of(blk * ROWS, ROWS), ROWS)

    def remote(src, dst, send, recv, device):
        return pltpu.make_async_remote_copy(
            src_ref=src, dst_ref=dst, send_sem=send, recv_sem=recv, device_id=device, device_id_type=MESH
        )

    kv_load = pltpu.make_async_copy(kv_hbm, kv_in, load_sem.at[0])
    q_load = pltpu.make_async_copy(q_hbm, q_in, load_sem.at[1])
    small = [
        pltpu.make_async_copy(src, dst, load_sem.at[3 + i])
        for i, (src, dst) in enumerate([(comp_hbm, comp_ref), (pos_hbm, pos_ref), (gain_hbm, gain_ref)])
    ]
    for load in small:
        load.start()
    kv_load.start()
    q_load.start()

    bar = pltpu.get_barrier_semaphore()

    def greet(k, carry):
        pl.semaphore_signal(
            bar, inc=1, device_id=in_plane((x + k // 4) % 4, (y + k % 4) % 4, b), device_id_type=MESH
        )
        return carry

    for d in range(1, NZ):
        pl.semaphore_signal(bar, inc=1, device_id=along_z(d), device_id_type=MESH)
    for d in (1, -1):

        @pl.when(jnp.logical_not(diagonal))
        def _():
            pl.semaphore_signal(bar, inc=1, device_id=partner_z(d), device_id_type=MESH)

    lax.fori_loop(1, 16, greet, 0)
    pl.semaphore_signal(bar, inc=1, device_id=sibling, device_id_type=MESH)

    @pl.when(jnp.logical_not(diagonal))
    def _():
        pl.semaphore_signal(bar, inc=1, device_id=partner, device_id_type=MESH)

    for load in small:
        load.wait()

    latent = comp_ref[:LAT, :].astype(jnp.float32).T
    normed = latent * lax.rsqrt(jnp.mean(latent * latent, axis=-1, keepdims=True) + 1e-06) * gain_ref[...]
    own = rows(ctx)
    packed[own, :LAT] = normed.astype(jnp.bfloat16)
    pos = pos_ref[...]
    high = jnp.broadcast_to((pos >> 6).astype(jnp.float32), (ROWS, ROWS)).T
    low = jnp.broadcast_to((pos & 63).astype(jnp.float32), (ROWS, ROWS)).T
    lane = lax.broadcasted_iota(jnp.int32, (ROWS, ROWS), 1)
    rope = comp_ref[LAT:, :].astype(jnp.float32)
    rope = jnp.concatenate([rope, rope], axis=0).T
    tail = jnp.where(lane < 64, rope, jnp.where(lane < 96, high, low))
    packed[own, LAT:] = tail.astype(jnp.bfloat16)

    pl.semaphore_wait(bar, jnp.where(diagonal, 23, 26))

    def far(n):
        return (z + jnp.where(n % 2 == 1, -((n + 1) // 2), n // 2) + NZ) % NZ

    w_swap = remote(w_hbm, w_both.at[a], w_send, w_recv, partner)
    w_load = pltpu.make_async_copy(w_hbm, w_both.at[b], load_sem.at[2])
    w_share = remote(w_both.at[b], w_both.at[b], w2_send, w2_recv, sibling)

    def piece(n, col, first, count):
        start = (far(n) * 2 + col) * ROWS + b * 64 + first
        return packed.at[pl.ds(pl.multiple_of(start, 32), count)]

    def from_far(n):
        d = (n + 1) // 2 if n % 2 == 1 else -(n // 2)
        hop = n in (5, 6)
        if hop:
            d = 1 if n == 5 else -1
        ref = piece(n - 2 if hop else 0, a, (y % 2) * 32, 32)
        return remote(ref, ref, far_send.at[n], far_recv.at[n], along_z(d))

    def from_near(k, n):
        ref = piece(n, a, (y % 2) * 32, 32)
        turn = 1 - 2 * b
        device = in_plane((x + 4 + turn * (k > 0)) % 4, (y + 4 + turn * (k != 1)) % 4, b)
        return remote(ref, ref, near_send.at[k, n], near_recv.at[k, n], device)

    def half(k, n):
        ref = piece(n, 1 - a if k else a, 0, 64)
        return remote(ref, ref, half_send.at[k, n], half_recv.at[k, n], sibling)

    def go(copies):
        for copy in copies:
            copy.start()

    def arrive(copies):
        for copy in copies:
            copy.wait_recv()

    go([from_far(n) for n in (1, 2, 3, 4, 7)])
    go([from_near(1, 0), from_near(2, 0)])

    @pl.when(jnp.logical_not(diagonal))
    def _():
        w_swap.start()

    @pl.when(diagonal)
    def _():
        w_load.start()

    kv_load.wait()
    for h in range(HEADS_DEV):
        kv_t[h] = kv_in[:, h * 256 + NOPE : (h + 1) * 256].astype(jnp.float32).T.astype(jnp.bfloat16)
    q_load.wait()
    for j in range(HEADS_DEV // 2):
        first = q_in[:, j * 384 : j * 384 + 128]
        second = q_in[:, j * 384 + 128 : j * 384 + 256].astype(jnp.float32)
        third = q_in[:, j * 384 + 256 : j * 384 + 384].astype(jnp.float32)
        second_turned = pltpu.roll(second, 64, 1)
        third_turned = pltpu.roll(third, 64, 1)
        qcat[2 * j, :, :NOPE] = first
        qcat[2 * j, :, NOPE:] = jnp.where(lane < 64, second, 0.0).astype(jnp.bfloat16)
        qcat[2 * j + 1, :, :NOPE] = jnp.where(lane < 64, second_turned, third_turned).astype(jnp.bfloat16)
        qcat[2 * j + 1, :, NOPE:] = jnp.where(lane < 64, third_turned, 0.0).astype(jnp.bfloat16)

    for h in range(HEADS_DEV):
        stats[h, 0:1, :] = jnp.full((1, ROWS), -1e30, jnp.float32)
        stats[h, 1:2, :] = jnp.zeros((1, ROWS), jnp.float32)
        acc[h] = jnp.zeros((VD, ROWS), jnp.float32)

    def attend(blk0, blk1, pairs):
        both = jnp.concatenate([packed[rows(blk0), :LAT], packed[rows(blk1), :LAT]], axis=0)
        extra = jnp.concatenate([packed[rows(blk0), LAT:], packed[rows(blk1), LAT:]], axis=0)
        wide = extra.astype(jnp.float32)
        key_pos = wide[:, 64:65] * 64.0 + wide[:, 96:97]
        bias = jnp.where(key_pos <= pos.astype(jnp.float32), 0.0, -1e30)
        heads = [2 * hp + i for hp in pairs for i in (0, 1)]
        ks, vs = {}, {}
        for hp in pairs:
            k_cols = jnp.concatenate([kv_in[:, hp * 512 + i * 256 : hp * 512 + i * 256 + NOPE] for i in (0, 1)], axis=1)
            ks[hp] = jnp.dot(both, k_cols, preferred_element_type=jnp.float32).astype(jnp.bfloat16)
            v_rows = jnp.concatenate([kv_t[hp * 2], kv_t[hp * 2 + 1]], axis=0)
            vs[hp] = lax.dot_general(v_rows, both, NT, preferred_element_type=jnp.float32).astype(jnp.bfloat16)
        scores, exps, fades = {}, {}, {}
        for h in heads:
            k_all = jnp.concatenate([ks[h // 2][:, h % 2 * 128 : h % 2 * 128 + 128], extra], axis=1)
            scores[h] = lax.dot_general(k_all, qcat[h], NT, preferred_element_type=jnp.float32) * SCALE + bias
        for h in heads:
            before = stats[h, 0:1, :]
            top = jnp.maximum(before, jnp.max(scores[h], axis=0, keepdims=True))
            fade = jnp.exp2(before - top)
            e = jnp.exp2(scores[h] - top)
            stats[h, 0:1, :] = top
            stats[h, 1:2, :] = stats[h, 1:2, :] * fade + jnp.sum(e, axis=0, keepdims=True)
            exps[h] = e.astype(jnp.bfloat16)
            fades[h] = fade
        for h in heads:
            v = vs[h // 2][h % 2 * 128 : h % 2 * 128 + 128, :]
            acc[h] = acc[h] * fades[h] + jnp.dot(v, exps[h], preferred_element_type=jnp.float32)

    def from_z(*ns):
        for n in ns:
            from_far(n).wait_recv()
            if n in (3, 4):
                from_far(n + 2).start()
            go([from_near(k, n) for k in range(3)])

    def from_plane(*ns):
        for n in ns:
            arrive([from_near(k, n) for k in range(3)])
            go([half(k, n) for k in (0, 1)])

    def before_stage(g):
        if g == 0:
            arrive([from_near(1, 0), from_near(2, 0)])
            half(1, 0).start()
            from_z(1, 2)
            half(1, 0).wait_recv()
        if g == 1:
            from_z(3, 4)
            from_plane(1, 2)
        if g == 2:
            from_z(5, 6)
        if g == 3:
            from_z(7)
            from_plane(3, 4)
        if g == 4:
            from_plane(5)
        if g == 5:
            from_plane(6)
        if g == 6:
            from_plane(7)
        if g > 0:
            arrive([half(k, g) for k in (0, 1)])

    def stage(g, carry):
        for k in range(NZ - 1):
            @pl.when(g == k)
            def _():
                before_stage(k)

        attend(far(g) * 2, far(g) * 2 + 1, range(HEADS_DEV // 2))
        return carry

    lax.fori_loop(0, NZ - 1, stage, 0)
    before_stage(NZ - 1)

    def ring(i, p, s):
        d = 1 if i == 0 else -1
        r = rows(block(-d * (s - 1), b))
        return remote(full.at[p, r], full.at[p, r], ring_send.at[i, p, s - 1], ring_recv.at[i, p, s - 1], along_z(d))

    def swap(p):
        return remote(att.at[p], full.at[p, own], swap_send.at[p], swap_recv.at[p], partner)

    def ring_first(i, p):
        return remote(
            att.at[p], full.at[p, own], ring_send.at[i, p, 0], ring_recv.at[i, p, 0], partner_z(1 if i == 0 else -1)
        )

    def pass_on(p, s):
        if s < 4:
            for i in (0, 1):
                ring(i, p, s).wait_recv()
                if s < 3 or i == p // 2:
                    ring(i, p, s + 1).start()
        else:
            ring(p // 2, p, 4).wait_recv()

    for p in range(CHUNKS):
        if p % 2 == 0:
            attend(far(NZ - 1) * 2, far(NZ - 1) * 2 + 1, (p, p + 1))
        for i in (0, 1):
            o = acc[2 * p + i] / stats[2 * p + i, 1:2, :]
            att[p, :, i * VD : (i + 1) * VD] = o.T.astype(jnp.bfloat16)
        ring_first(0, p).start()
        ring_first(1, p).start()

        @pl.when(diagonal)
        def _():
            full[p, own, :] = att[p]

    @pl.when(jnp.logical_not(diagonal))
    def _():
        for p in range(CHUNKS):
            swap(p).start()

    @pl.when(diagonal)
    def _():
        w_load.wait()

    @pl.when(jnp.logical_not(diagonal))
    def _():
        w_swap.wait_recv()

    w_share.start()
    for p in range(CHUNKS):
        pass_on(p, 1)

    u = jnp.where(b == 0, y, x)
    v = jnp.where(b == 0, x, y)

    def first_copy(n, j):
        t = (u + j) % 4
        device = in_plane(jnp.where(b == 0, x, t), jnp.where(b == 0, t, y), b)
        src = part.at[n, pl.ds(pl.multiple_of(t * 64, 64), 64)]
        return remote(src, got1.at[n, j - 1], first_send.at[n, j - 1], first_recv.at[n, j - 1], device)

    def second_copy(n, j):
        t = (v + j) % 4
        device = in_plane(jnp.where(b == 0, t, x), jnp.where(b == 0, y, t), b)
        src = sum1.at[n, pl.ds(pl.multiple_of(t * 16, 16), 16)]
        return remote(src, got2.at[n, j - 1], second_send.at[n, j - 1], second_recv.at[n, j - 1], device)

    def project(n, carry):
        r = rows(far(n) * 2 + b)
        lhs = jnp.concatenate([full[p, r, :] for p in range(CHUNKS)], axis=1)
        for i in (0, 1):
            part[n, i * ROWS : (i + 1) * ROWS, :] = lax.dot_general(
                lhs, w_both[i], NT, preferred_element_type=jnp.float32
            ).astype(jnp.bfloat16)
        for j in (1, 2, 3):
            first_copy(n, j).start()
        return carry

    def sum_first(n, carry):
        total = part[n, pl.ds(pl.multiple_of(u * 64, 64), 64), :].astype(jnp.float32)
        for j in (1, 2, 3):
            first_copy(n, j).wait_recv()
        for j in (1, 2, 3):
            total = total + got1[n, j - 1].astype(jnp.float32)
        sum1[n] = total.astype(jnp.bfloat16)
        for j in (1, 2, 3):
            second_copy(n, j).start()
        return carry

    slot = (u % 2) * 4 + v

    def last_copy(n):
        zp = far(n)
        device = in_plane((zp // 4) * 2 + u // 2, zp % 4, b)
        return remote(
            sum2.at[n], result.at[pl.ds(pl.multiple_of(slot * 16, 16), 16)], last_send.at[n], last_recv.at[slot], device
        )

    def stays(n):
        zp = far(n)
        return (u // 2 == a) & (zp == xh * 4 + y)

    def sum_second(n, carry):
        total = sum1[n, pl.ds(pl.multiple_of(v * 16, 16), 16), :].astype(jnp.float32)
        for j in (1, 2, 3):
            second_copy(n, j).wait_recv()
        for j in (1, 2, 3):
            total = total + got2[n, j - 1].astype(jnp.float32)
        sum2[n] = total.astype(jnp.bfloat16)

        @pl.when(stays(n))
        def _():
            result[pl.ds(pl.multiple_of(slot * 16, 16), 16), :] = sum2[n]

        @pl.when(jnp.logical_not(stays(n)))
        def _():
            last_copy(n).start()

        return carry

    def project_round(s):
        lax.fori_loop(2 * s - 1, 2 * s + 1, project, 0)

    pass_on(0, 2)
    w_share.wait_recv()

    @pl.when(jnp.logical_not(diagonal))
    def _():
        for p in range(CHUNKS):
            swap(p).wait_recv()

    project(0, 0)

    for n in range(NZ):
        for k in range(3):
            if n > 0 or k > 0:
                from_near(k, n).wait_send()
        for k in (0, 1):
            if n > 0 or k > 0:
                half(k, n).wait_send()
        if n > 0:
            from_far(n).wait_send()

    @pl.when(jnp.logical_not(diagonal))
    def _():
        w_swap.wait_send()
        for p in range(CHUNKS):
            swap(p).wait_send()

    pass_on(1, 2)
    project_round(1)
    pass_on(2, 2)
    pass_on(3, 2)
    pass_on(0, 3)
    pass_on(1, 3)
    project_round(2)
    pass_on(2, 3)
    lax.fori_loop(0, 3, sum_first, 0)
    pass_on(3, 3)
    project_round(3)
    pass_on(0, 4)
    pass_on(2, 4)
    lax.fori_loop(3, 5, sum_first, 0)
    lax.fori_loop(0, 3, sum_second, 0)
    pass_on(1, 4)
    pass_on(3, 4)
    project(7, 0)
    w_share.wait_send()
    for p in range(CHUNKS):
        for i in (0, 1):
            for s in (1, 2, 3):
                ring(i, p, s).wait_send()
        ring(p // 2, p, 4).wait_send()
    lax.fori_loop(5, 7, sum_first, 0)
    lax.fori_loop(3, 5, sum_second, 0)
    sum_first(7, 0)

    def first_left(n, carry):
        for j in (1, 2, 3):
            first_copy(n, j).wait_send()
        return carry

    def second_left(n, carry):
        for j in (1, 2, 3):
            second_copy(n, j).wait_send()
        return carry

    lax.fori_loop(0, NZ, first_left, 0)
    lax.fori_loop(5, 8, sum_second, 0)
    lax.fori_loop(0, NZ, second_left, 0)

    for n in range(8):
        un = a * 2 + n // 4
        mine = (un == u) & (n % 4 == v)

        @pl.when(jnp.logical_not(mine))
        def _():
            remote(sum2.at[0], result.at[pl.ds(n * 16, 16)], last_send.at[0], last_recv.at[n], sibling).wait_recv()

    out_ref[...] = result[...].astype(jnp.float32).T.astype(jnp.bfloat16)

    for n in range(NZ):
        @pl.when(jnp.logical_not(stays(n)))
        def _():
            last_copy(n).wait_send()


def per_device(queries, compressed, kv_up, w_out, positions, latent_gain):
    bf16, f32 = jnp.bfloat16, jnp.float32
    dma = pltpu.SemaphoreType.DMA
    any_space = pl.BlockSpec(memory_space=pl.ANY)
    vmem = pl.BlockSpec(memory_space=pltpu.VMEM)
    return pl.pallas_call(
        kernel,
        out_shape=jax.ShapeDtypeStruct((COLS, ROWS), bf16),
        in_specs=[any_space] * 6,
        out_specs=vmem,
        scratch_shapes=[
            pltpu.VMEM((LAT + ROPE, ROWS), bf16),
            pltpu.VMEM((1, ROWS), jnp.int32),
            pltpu.VMEM((1, LAT), f32),
            pltpu.VMEM((NZ * 2 * ROWS, WIDE), bf16),
            pltpu.VMEM((HEADS_DEV, ROWS, 256), bf16),
            pltpu.VMEM((ROWS, HEADS_DEV * QK), bf16),
            pltpu.VMEM((LAT, HEADS_DEV * 256), bf16),
            pltpu.VMEM((HEADS_DEV, VD, LAT), bf16),
            pltpu.VMEM((HEADS_DEV, 8, ROWS), f32),
            pltpu.VMEM((HEADS_DEV, VD, ROWS), f32),
            pltpu.VMEM((CHUNKS, ROWS, 256), bf16),
            pltpu.VMEM((CHUNKS, NZ * 2 * ROWS, 256), bf16),
            pltpu.VMEM((2, COLS, HEADS_DEV * VD), bf16),
            pltpu.VMEM((NZ, 2 * ROWS, COLS), bf16),
            pltpu.VMEM((NZ, 3, 64, COLS), bf16),
            pltpu.VMEM((NZ, 64, COLS), bf16),
            pltpu.VMEM((NZ, 3, 16, COLS), bf16),
            pltpu.VMEM((NZ, 16, COLS), bf16),
            pltpu.VMEM((ROWS, COLS), bf16),
            dma((NZ,)), dma((NZ,)),
            dma((3, NZ)), dma((3, NZ)),
            dma((2, NZ)), dma((2, NZ)),
            dma, dma,
            dma, dma,
            dma((6,)),
            dma((2, CHUNKS, 4)), dma((2, CHUNKS, 4)),
            dma((CHUNKS,)), dma((CHUNKS,)),
            dma((NZ, 3)), dma((NZ, 3)),
            dma((NZ, 3)), dma((NZ, 3)),
            dma((NZ,)), dma((NZ,)),
        ],
        compiler_params=pltpu.CompilerParams(
            collective_id=0, has_side_effects=True, vmem_limit_bytes=56 * 1024 * 1024
        ),
        name="prefill",
    )(queries, compressed.T, kv_up, w_out.T, positions.reshape(1, ROWS), latent_gain.reshape(1, LAT)).T


def solution(mesh):
    in_specs = (P("ctx", "head"), P("ctx", None), P(None, "head"), P("head", "ctx"), P("ctx"), P())
    return jax.shard_map(
        per_device, mesh=mesh, in_specs=in_specs, out_specs=P("head", "ctx"), check_vma=False
    )
```

```python
import math

import jax
import jax.numpy as jnp
from jax import lax
from jax.experimental import pallas as pl
from jax.experimental.pallas import tpu as pltpu
from jax.sharding import PartitionSpec as P

LAT = 512
NOPE = 128
ROPE = 64
VD = 128
QK = 192
WIDE = 640
ROWS = 128
HEADS_DEV = 8
CHUNKS = 4
NZ = 8
COLS = 448
MESH = pl.DeviceIdType.MESH
SCALE = math.log2(math.e) / math.sqrt(QK)
NT = (((1,), (1,)), ((), ()))


def kernel(
    q_hbm, comp_hbm, kv_hbm, w_hbm, pos_hbm, gain_hbm, out_ref,
    comp_ref, pos_ref, gain_ref, packed, qcat, q_in, kv_in, kv_t, stats, acc, att, full, w_both, part, got1, sum1, got2, sum2, result,
    far_send, far_recv, near_send, near_recv, half_send, half_recv,
    w_send, w_recv, w2_send, w2_recv, load_sem,
    ring_send, ring_recv, swap_send, swap_recv,
    first_send, first_recv, second_send, second_recv, last_send, last_recv,
):
    ctx, head = lax.axis_index("ctx"), lax.axis_index("head")
    z, a = ctx // 2, ctx % 2
    xh, y, b = head // 8, (head // 2) % 4, head % 2
    x = xh * 2 + a
    diagonal = a == b
    partner = (z * 2 + b, xh * 8 + y * 2 + a)
    sibling = (ctx, xh * 8 + y * 2 + (1 - b))

    def along_z(d):
        return (((z + d + NZ) % NZ) * 2 + a, head)

    def partner_z(d):
        return (((z + d + NZ) % NZ) * 2 + b, xh * 8 + y * 2 + a)

    def in_plane(px, py, core):
        return (z * 2 + px % 2, (px // 2) * 8 + py * 2 + core)

    def block(dz, core):
        return ((z + dz + 2 * NZ) % NZ) * 2 + core

    def rows(blk):
        return pl.ds(pl.multiple_of(blk * ROWS, ROWS), ROWS)

    def remote(src, dst, send, recv, device):
        return pltpu.make_async_remote_copy(
            src_ref=src, dst_ref=dst, send_sem=send, recv_sem=recv, device_id=device, device_id_type=MESH
        )

    kv_load = pltpu.make_async_copy(kv_hbm, kv_in, load_sem.at[0])
    q_load = pltpu.make_async_copy(q_hbm, q_in, load_sem.at[1])
    small = [
        pltpu.make_async_copy(src, dst, load_sem.at[3 + i])
        for i, (src, dst) in enumerate([(comp_hbm, comp_ref), (pos_hbm, pos_ref), (gain_hbm, gain_ref)])
    ]
    for load in small:
        load.start()
    kv_load.start()
    q_load.start()

    bar = pltpu.get_barrier_semaphore()

    def greet(k, carry):
        pl.semaphore_signal(
            bar, inc=1, device_id=in_plane((x + k // 4) % 4, (y + k % 4) % 4, b), device_id_type=MESH
        )
        return carry

    for d in range(1, NZ):
        pl.semaphore_signal(bar, inc=1, device_id=along_z(d), device_id_type=MESH)
    for d in (1, -1):

        @pl.when(jnp.logical_not(diagonal))
        def _():
            pl.semaphore_signal(bar, inc=1, device_id=partner_z(d), device_id_type=MESH)

    lax.fori_loop(1, 16, greet, 0)
    pl.semaphore_signal(bar, inc=1, device_id=sibling, device_id_type=MESH)

    @pl.when(jnp.logical_not(diagonal))
    def _():
        pl.semaphore_signal(bar, inc=1, device_id=partner, device_id_type=MESH)

    for load in small:
        load.wait()

    latent = comp_ref[:LAT, :].astype(jnp.float32).T
    normed = latent * lax.rsqrt(jnp.mean(latent * latent, axis=-1, keepdims=True) + 1e-06) * gain_ref[...]
    own = rows(ctx)
    packed[own, :LAT] = normed.astype(jnp.bfloat16)
    pos = pos_ref[...]
    high = jnp.broadcast_to((pos >> 6).astype(jnp.float32), (ROWS, ROWS)).T
    low = jnp.broadcast_to((pos & 63).astype(jnp.float32), (ROWS, ROWS)).T
    lane = lax.broadcasted_iota(jnp.int32, (ROWS, ROWS), 1)
    rope = comp_ref[LAT:, :].astype(jnp.float32)
    rope = jnp.concatenate([rope, rope], axis=0).T
    tail = jnp.where(lane < 64, rope, jnp.where(lane < 96, high, low))
    packed[own, LAT:] = tail.astype(jnp.bfloat16)

    pl.semaphore_wait(bar, jnp.where(diagonal, 23, 26))

    def far(n):
        return (z + jnp.where(n % 2 == 1, -((n + 1) // 2), n // 2) + NZ) % NZ

    w_swap = remote(w_hbm, w_both.at[a], w_send, w_recv, partner)
    w_load = pltpu.make_async_copy(w_hbm, w_both.at[b], load_sem.at[2])
    w_share = remote(w_both.at[b], w_both.at[b], w2_send, w2_recv, sibling)

    def piece(n, col, first, count):
        start = (far(n) * 2 + col) * ROWS + b * 64 + first
        return packed.at[pl.ds(pl.multiple_of(start, 32), count)]

    def from_far(n):
        d = (n + 1) // 2 if n % 2 == 1 else -(n // 2)
        hop = n in (5, 6)
        if hop:
            d = 1 if n == 5 else -1
        ref = piece(n - 2 if hop else 0, a, (y % 2) * 32, 32)
        return remote(ref, ref, far_send.at[n], far_recv.at[n], along_z(d))

    def from_near(k, n):
        ref = piece(n, a, (y % 2) * 32, 32)
        turn = 1 - 2 * b
        device = in_plane((x + 4 + turn * (k > 0)) % 4, (y + 4 + turn * (k != 1)) % 4, b)
        return remote(ref, ref, near_send.at[k, n], near_recv.at[k, n], device)

    def half(k, n):
        ref = piece(n, 1 - a if k else a, 0, 64)
        return remote(ref, ref, half_send.at[k, n], half_recv.at[k, n], sibling)

    def go(copies):
        for copy in copies:
            copy.start()

    def arrive(copies):
        for copy in copies:
            copy.wait_recv()

    go([from_far(n) for n in (1, 2, 3, 4, 7)])
    go([from_near(1, 0), from_near(2, 0)])

    @pl.when(jnp.logical_not(diagonal))
    def _():
        w_swap.start()

    @pl.when(diagonal)
    def _():
        w_load.start()

    kv_load.wait()
    for h in range(HEADS_DEV):
        kv_t[h] = kv_in[:, h * 256 + NOPE : (h + 1) * 256].astype(jnp.float32).T.astype(jnp.bfloat16)
    q_load.wait()
    for j in range(HEADS_DEV // 2):
        first = q_in[:, j * 384 : j * 384 + 128]
        second = q_in[:, j * 384 + 128 : j * 384 + 256].astype(jnp.float32)
        third = q_in[:, j * 384 + 256 : j * 384 + 384].astype(jnp.float32)
        second_turned = pltpu.roll(second, 64, 1)
        third_turned = pltpu.roll(third, 64, 1)
        qcat[2 * j, :, :NOPE] = first
        qcat[2 * j, :, NOPE:] = jnp.where(lane < 64, second, 0.0).astype(jnp.bfloat16)
        qcat[2 * j + 1, :, :NOPE] = jnp.where(lane < 64, second_turned, third_turned).astype(jnp.bfloat16)
        qcat[2 * j + 1, :, NOPE:] = jnp.where(lane < 64, third_turned, 0.0).astype(jnp.bfloat16)

    for h in range(HEADS_DEV):
        stats[h, 0:1, :] = jnp.full((1, ROWS), -1e30, jnp.float32)
        stats[h, 1:2, :] = jnp.zeros((1, ROWS), jnp.float32)
        acc[h] = jnp.zeros((VD, ROWS), jnp.float32)

    def attend(blk0, blk1, pairs):
        both = jnp.concatenate([packed[rows(blk0), :LAT], packed[rows(blk1), :LAT]], axis=0)
        extra = jnp.concatenate([packed[rows(blk0), LAT:], packed[rows(blk1), LAT:]], axis=0)
        wide = extra.astype(jnp.float32)
        key_pos = wide[:, 64:65] * 64.0 + wide[:, 96:97]
        bias = jnp.where(key_pos <= pos.astype(jnp.float32), 0.0, -1e30)
        heads = [2 * hp + i for hp in pairs for i in (0, 1)]
        ks, vs = {}, {}
        for hp in pairs:
            k_cols = jnp.concatenate([kv_in[:, hp * 512 + i * 256 : hp * 512 + i * 256 + NOPE] for i in (0, 1)], axis=1)
            ks[hp] = jnp.dot(both, k_cols, preferred_element_type=jnp.float32).astype(jnp.bfloat16)
            v_rows = jnp.concatenate([kv_t[hp * 2], kv_t[hp * 2 + 1]], axis=0)
            vs[hp] = lax.dot_general(v_rows, both, NT, preferred_element_type=jnp.float32).astype(jnp.bfloat16)
        scores, exps, fades = {}, {}, {}
        for h in heads:
            k_all = jnp.concatenate([ks[h // 2][:, h % 2 * 128 : h % 2 * 128 + 128], extra], axis=1)
            scores[h] = lax.dot_general(k_all, qcat[h], NT, preferred_element_type=jnp.float32) * SCALE + bias
        for h in heads:
            before = stats[h, 0:1, :]
            top = jnp.maximum(before, jnp.max(scores[h], axis=0, keepdims=True))
            fade = jnp.exp2(before - top)
            e = jnp.exp2(scores[h] - top)
            stats[h, 0:1, :] = top
            stats[h, 1:2, :] = stats[h, 1:2, :] * fade + jnp.sum(e, axis=0, keepdims=True)
            exps[h] = e.astype(jnp.bfloat16)
            fades[h] = fade
        for h in heads:
            v = vs[h // 2][h % 2 * 128 : h % 2 * 128 + 128, :]
            acc[h] = acc[h] * fades[h] + jnp.dot(v, exps[h], preferred_element_type=jnp.float32)

    def from_z(*ns):
        for n in ns:
            from_far(n).wait_recv()
            if n in (3, 4):
                from_far(n + 2).start()
            go([from_near(k, n) for k in range(3)])

    def from_plane(*ns):
        for n in ns:
            arrive([from_near(k, n) for k in range(3)])
            go([half(k, n) for k in (0, 1)])

    def before_stage(g):
        if g == 0:
            arrive([from_near(1, 0), from_near(2, 0)])
            half(1, 0).start()
            from_z(1, 2)
            half(1, 0).wait_recv()
        if g == 1:
            from_z(3, 4)
            from_plane(1, 2)
        if g == 2:
            from_z(5, 6)
        if g == 3:
            from_z(7)
            from_plane(3, 4)
        if g == 4:
            from_plane(5)
        if g == 5:
            from_plane(6)
        if g == 6:
            from_plane(7)
        if g > 0:
            arrive([half(k, g) for k in (0, 1)])

    def stage(g, carry):
        for k in range(NZ - 1):
            @pl.when(g == k)
            def _():
                before_stage(k)

        attend(far(g) * 2, far(g) * 2 + 1, range(HEADS_DEV // 2))
        return carry

    lax.fori_loop(0, NZ - 1, stage, 0)
    before_stage(NZ - 1)

    def ring(i, p, s):
        d = 1 if i == 0 else -1
        r = rows(block(-d * (s - 1), b))
        return remote(full.at[p, r], full.at[p, r], ring_send.at[i, p, s - 1], ring_recv.at[i, p, s - 1], along_z(d))

    def swap(p):
        return remote(att.at[p], full.at[p, own], swap_send.at[p], swap_recv.at[p], partner)

    def ring_first(i, p):
        return remote(
            att.at[p], full.at[p, own], ring_send.at[i, p, 0], ring_recv.at[i, p, 0], partner_z(1 if i == 0 else -1)
        )

    def pass_on(p, s):
        if s < 4:
            for i in (0, 1):
                ring(i, p, s).wait_recv()
                if s < 3 or i == p // 2:
                    ring(i, p, s + 1).start()
        else:
            ring(p // 2, p, 4).wait_recv()

    for p in range(CHUNKS):
        if p % 2 == 0:
            attend(far(NZ - 1) * 2, far(NZ - 1) * 2 + 1, (p, p + 1))
        for i in (0, 1):
            o = acc[2 * p + i] / stats[2 * p + i, 1:2, :]
            att[p, :, i * VD : (i + 1) * VD] = o.T.astype(jnp.bfloat16)
        ring_first(0, p).start()
        ring_first(1, p).start()

        @pl.when(diagonal)
        def _():
            full[p, own, :] = att[p]

    @pl.when(jnp.logical_not(diagonal))
    def _():
        for p in range(CHUNKS):
            swap(p).start()

    @pl.when(diagonal)
    def _():
        w_load.wait()

    @pl.when(jnp.logical_not(diagonal))
    def _():
        w_swap.wait_recv()

    w_share.start()
    for p in range(CHUNKS):
        pass_on(p, 1)

    u = jnp.where(b == 0, y, x)
    v = jnp.where(b == 0, x, y)

    def first_copy(n, j):
        t = (u + j) % 4
        device = in_plane(jnp.where(b == 0, x, t), jnp.where(b == 0, t, y), b)
        src = part.at[n, pl.ds(pl.multiple_of(t * 64, 64), 64)]
        return remote(src, got1.at[n, j - 1], first_send.at[n, j - 1], first_recv.at[n, j - 1], device)

    def second_copy(n, j):
        t = (v + j) % 4
        device = in_plane(jnp.where(b == 0, t, x), jnp.where(b == 0, y, t), b)
        src = sum1.at[n, pl.ds(pl.multiple_of(t * 16, 16), 16)]
        return remote(src, got2.at[n, j - 1], second_send.at[n, j - 1], second_recv.at[n, j - 1], device)

    def project(n, carry):
        r = rows(far(n) * 2 + b)
        lhs = jnp.concatenate([full[p, r, :] for p in range(CHUNKS)], axis=1)
        for i in (0, 1):
            part[n, i * ROWS : (i + 1) * ROWS, :] = lax.dot_general(
                lhs, w_both[i], NT, preferred_element_type=jnp.float32
            ).astype(jnp.bfloat16)
        for j in (1, 2, 3):
            first_copy(n, j).start()
        return carry

    def sum_first(n, carry):
        total = part[n, pl.ds(pl.multiple_of(u * 64, 64), 64), :].astype(jnp.float32)
        for j in (1, 2, 3):
            first_copy(n, j).wait_recv()
        for j in (1, 2, 3):
            total = total + got1[n, j - 1].astype(jnp.float32)
        sum1[n] = total.astype(jnp.bfloat16)
        for j in (1, 2, 3):
            second_copy(n, j).start()
        return carry

    slot = (u % 2) * 4 + v

    def last_copy(n):
        zp = far(n)
        device = in_plane((zp // 4) * 2 + u // 2, zp % 4, b)
        return remote(
            sum2.at[n], result.at[pl.ds(pl.multiple_of(slot * 16, 16), 16)], last_send.at[n], last_recv.at[slot], device
        )

    def stays(n):
        zp = far(n)
        return (u // 2 == a) & (zp == xh * 4 + y)

    def sum_second(n, carry):
        total = sum1[n, pl.ds(pl.multiple_of(v * 16, 16), 16), :].astype(jnp.float32)
        for j in (1, 2, 3):
            second_copy(n, j).wait_recv()
        for j in (1, 2, 3):
            total = total + got2[n, j - 1].astype(jnp.float32)
        sum2[n] = total.astype(jnp.bfloat16)

        @pl.when(stays(n))
        def _():
            result[pl.ds(pl.multiple_of(slot * 16, 16), 16), :] = sum2[n]

        @pl.when(jnp.logical_not(stays(n)))
        def _():
            last_copy(n).start()

        return carry

    def project_round(s):
        lax.fori_loop(2 * s - 1, 2 * s + 1, project, 0)

    pass_on(0, 2)
    w_share.wait_recv()

    @pl.when(jnp.logical_not(diagonal))
    def _():
        for p in range(CHUNKS):
            swap(p).wait_recv()

    project(0, 0)

    for n in range(NZ):
        for k in range(3):
            if n > 0 or k > 0:
                from_near(k, n).wait_send()
        for k in (0, 1):
            if n > 0 or k > 0:
                half(k, n).wait_send()
        if n > 0:
            from_far(n).wait_send()

    @pl.when(jnp.logical_not(diagonal))
    def _():
        w_swap.wait_send()
        for p in range(CHUNKS):
            swap(p).wait_send()

    pass_on(1, 2)
    project_round(1)
    pass_on(2, 2)
    pass_on(3, 2)
    pass_on(0, 3)
    pass_on(1, 3)
    project_round(2)
    pass_on(2, 3)
    lax.fori_loop(0, 3, sum_first, 0)
    pass_on(3, 3)
    project_round(3)
    pass_on(0, 4)
    pass_on(2, 4)
    lax.fori_loop(3, 5, sum_first, 0)
    lax.fori_loop(0, 3, sum_second, 0)
    pass_on(1, 4)
    pass_on(3, 4)
    project(7, 0)
    w_share.wait_send()
    for p in range(CHUNKS):
        for i in (0, 1):
            for s in (1, 2, 3):
                ring(i, p, s).wait_send()
        ring(p // 2, p, 4).wait_send()
    lax.fori_loop(5, 7, sum_first, 0)
    lax.fori_loop(3, 5, sum_second, 0)
    sum_first(7, 0)

    def first_left(n, carry):
        for j in (1, 2, 3):
            first_copy(n, j).wait_send()
        return carry

    def second_left(n, carry):
        for j in (1, 2, 3):
            second_copy(n, j).wait_send()
        return carry

    lax.fori_loop(0, NZ, first_left, 0)
    lax.fori_loop(5, 8, sum_second, 0)
    lax.fori_loop(0, NZ, second_left, 0)

    for n in range(8):
        un = a * 2 + n // 4
        mine = (un == u) & (n % 4 == v)

        @pl.when(jnp.logical_not(mine))
        def _():
            remote(sum2.at[0], result.at[pl.ds(n * 16, 16)], last_send.at[0], last_recv.at[n], sibling).wait_recv()

    out_ref[...] = result[...]

    for n in range(NZ):
        @pl.when(jnp.logical_not(stays(n)))
        def _():
            last_copy(n).wait_send()


def per_device(queries, compressed, kv_up, w_out, positions, latent_gain):
    bf16, f32 = jnp.bfloat16, jnp.float32
    dma = pltpu.SemaphoreType.DMA
    any_space = pl.BlockSpec(memory_space=pl.ANY)
    vmem = pl.BlockSpec(memory_space=pltpu.VMEM)
    return pl.pallas_call(
        kernel,
        out_shape=jax.ShapeDtypeStruct((ROWS, COLS), bf16),
        in_specs=[any_space] * 6,
        out_specs=vmem,
        scratch_shapes=[
            pltpu.VMEM((LAT + ROPE, ROWS), bf16),
            pltpu.VMEM((1, ROWS), jnp.int32),
            pltpu.VMEM((1, LAT), f32),
            pltpu.VMEM((NZ * 2 * ROWS, WIDE), bf16),
            pltpu.VMEM((HEADS_DEV, ROWS, 256), bf16),
            pltpu.VMEM((ROWS, HEADS_DEV * QK), bf16),
            pltpu.VMEM((LAT, HEADS_DEV * 256), bf16),
            pltpu.VMEM((HEADS_DEV, VD, LAT), bf16),
            pltpu.VMEM((HEADS_DEV, 8, ROWS), f32),
            pltpu.VMEM((HEADS_DEV, VD, ROWS), f32),
            pltpu.VMEM((CHUNKS, ROWS, 256), bf16),
            pltpu.VMEM((CHUNKS, NZ * 2 * ROWS, 256), bf16),
            pltpu.VMEM((2, COLS, HEADS_DEV * VD), bf16),
            pltpu.VMEM((NZ, 2 * ROWS, COLS), bf16),
            pltpu.VMEM((NZ, 3, 64, COLS), bf16),
            pltpu.VMEM((NZ, 64, COLS), bf16),
            pltpu.VMEM((NZ, 3, 16, COLS), bf16),
            pltpu.VMEM((NZ, 16, COLS), bf16),
            pltpu.VMEM((ROWS, COLS), bf16),
            dma((NZ,)), dma((NZ,)),
            dma((3, NZ)), dma((3, NZ)),
            dma((2, NZ)), dma((2, NZ)),
            dma, dma,
            dma, dma,
            dma((6,)),
            dma((2, CHUNKS, 4)), dma((2, CHUNKS, 4)),
            dma((CHUNKS,)), dma((CHUNKS,)),
            dma((NZ, 3)), dma((NZ, 3)),
            dma((NZ, 3)), dma((NZ, 3)),
            dma((NZ,)), dma((NZ,)),
        ],
        compiler_params=pltpu.CompilerParams(
            collective_id=0, has_side_effects=True, vmem_limit_bytes=56 * 1024 * 1024
        ),
        name="prefill",
    )(queries, compressed.T, kv_up, w_out.T, positions.reshape(1, ROWS), latent_gain.reshape(1, LAT))


def solution(mesh):
    in_specs = (P("ctx", "head"), P("ctx", None), P(None, "head"), P("head", "ctx"), P("ctx"), P())
    return jax.shard_map(
        per_device, mesh=mesh, in_specs=in_specs, out_specs=P("head", "ctx"), check_vma=False
    )
```
